32 devices in a mesh: prow: 4 (over z), pcol: 8 (over y, x, core).
Axes of the slice: x: 2, y: 2, z: 4, core: 2. Of those that a mesh axis runs over, the one named last changes fastest.
Arguments:
- matrix: bfloat16 [3, 2048, 1, 4096], P(None, 'prow', None, 'pcol'), may hold values from -6 to 6
- pattern: int32 [12, 8], replicated, may hold values 0 or 1
- inverses: bfloat16 [2, 512, 512], replicated, may hold values from -0.01171875 to 0.01171875
- pivots: int32 [2, 3], replicated, may hold values from 0 to 11, as said below
Outputs:
- factored: bfloat16 [3, 2048, 1, 4096], P(None, 'prow', None, 'pcol')
The draws below stay inside these ranges and needn't reach their ends.
Inputs may be any that keep to these rules, and one draw needn't show every extreme that they name: pivots[s] = (a, b, c) with a and b block rows in 0 .. 11 and c a block column in 0 .. 7; the 4 numbers a and b over all steps are all different, and so are the 2 numbers c; b mod 4 = (a + 2) mod 4 for every step; block row 0 and block row 11 are among the b, and block column 7 is among the c.
All inputs are finite; a program needn't handle non-finite values.
Results may differ from the reference program's by a relative error of at most 0.0068.
Values may be sent and summed in bfloat16 or wider, within the bound.
No kernel may reach another device: no remote copies, remote signals or barrier semaphores. Data moves between devices by JAX's collectives and lax.ppermute only.
A program may use at most 64 MiB of HBM per device.

```python
import jax
import jax.numpy as jnp
from jax import lax

NB = 512
RB_DEV = 3
CB_DEV = 1
STEPS = 2
MB = 12
NC = 8
N_PROW = 4
N_PCOL = 8


def draw_pivots(key, part):
    half_axis = N_PROW // 2
    step_ids = jnp.arange(STEPS, dtype=jnp.int32)
    owner_second = jnp.where(step_ids == 0, 0, jnp.where(step_ids == STEPS - 1, N_PROW - 1, step_ids)).astype(jnp.int32)
    owner_first = ((owner_second + half_axis) % N_PROW).astype(jnp.int32)
    slots_first = jax.random.randint(jax.random.fold_in(key, 11), (STEPS,), 0, RB_DEV).astype(jnp.int32)
    slots_other = jax.random.randint(jax.random.fold_in(key, 13), (STEPS,), 0, RB_DEV).astype(jnp.int32)
    slots_second = jnp.where(step_ids == 0, 0, jnp.where(step_ids == STEPS - 1, RB_DEV - 1, slots_other)).astype(jnp.int32)
    firsts = (slots_first * N_PROW + owner_first).astype(jnp.int32)
    seconds = (slots_second * N_PROW + owner_second).astype(jnp.int32)
    others = jax.random.permutation(jax.random.fold_in(key, 12), NC - 1)[:STEPS - 1]
    cols = jnp.concatenate([others.astype(jnp.int32), jnp.full((1,), NC - 1, jnp.int32)])
    return jnp.stack([firsts, seconds, cols], axis=1).astype(jnp.int32)


def with_ends(result, stream_key, low, largest):
    longest = result.shape.index(max(result.shape))
    spots = []
    for shift in (0, 1):
        where = [jax.random.randint(jax.random.fold_in(stream_key, axis), (), 0, length) for axis, length in enumerate(result.shape)]
        where[longest] = (where[longest] + shift) % result.shape[longest]
        spots.append(tuple(where))
    return result.at[spots[0]].set(low).at[spots[1]].set(largest)


def block_levels(rng, shape, cuts, least, largest):
    loudness, own = 1.0, jax.random.fold_in(rng, 6)
    for position, blocks in cuts:
        heights = jnp.exp(jax.random.uniform(jax.random.fold_in(own, position), (blocks,), jnp.float32, least / len(cuts), largest / len(cuts)))
        loudness = loudness * jnp.repeat(heights, shape[position] // blocks).reshape([-1 if axis == position else 1 for axis in range(len(shape))])
    return loudness


def centred(stream_key, extent, spread, most, pieces=(), held_as=jnp.bfloat16):
    drawn = spread * jax.random.normal(stream_key, extent, jnp.float32)
    if pieces:
        drawn = drawn * block_levels(stream_key, extent, pieces, -0.22, 0.18)
    return jnp.clip(drawn, -most, most).astype(held_as)


def setup_inputs(seed: int = 0) -> dict:
    key_list = jax.random.split(jax.random.key(seed), 5)
    matrix = centred(key_list[0], (RB_DEV, NB * N_PROW, CB_DEV, NB * N_PCOL), 1.0, 6.0, ((1, 4), (3, 8)))
    pattern = with_ends((jax.random.randint(key_list[1], (MB, NC), 0, 4) < 3).astype(jnp.int32), jax.random.fold_in(key_list[1], 1), 0, 1)
    inverses = centred(key_list[2], (STEPS, NB, NB), (NB * NB) ** -0.5, 0.01171875)
    pivots = draw_pivots(jax.random.fold_in(key_list[4], 71), 0)
    return {"matrix": matrix, "pattern": pattern, "inverses": inverses, "pivots": pivots}


def reference(matrix, pattern, inverses, pivots):
    blocks = matrix.reshape(MB, NB, NC, NB)
    keep = pattern.astype(matrix.dtype)
    work = blocks * keep[:, None, :, None]
    row_ids = jnp.arange(MB, dtype=jnp.int32)
    col_ids = jnp.arange(NC, dtype=jnp.int32)
    for step in range(STEPS):
        first = pivots[step, 0]
        second = pivots[step, 1]
        column_id = pivots[step, 2]
        row_first = work[first]
        row_second = work[second]
        work = work.at[first].set(row_second)
        work = work.at[second].set(row_first)
        column = work[:, :, column_id, :]
        multipliers = jnp.dot(column.reshape(MB * NB, NB), inverses[step], preferred_element_type=jnp.float32)
        multipliers = multipliers.astype(matrix.dtype).reshape(MB, NB, NB)
        upper = work[first].reshape(NB, NC * NB)
        live_rows = jnp.all(row_ids[:, None] != pivots[None, :step + 1, 0], axis=1)
        live_cols = jnp.all(col_ids[:, None] != pivots[None, :step + 1, 2], axis=1)
        is_column = col_ids == column_id

        def update(item):
            old, left, live = item
            product = jnp.dot(left, upper, preferred_element_type=jnp.float32).reshape(NB, NC, NB)
            fresh = (old.astype(jnp.float32) - product).astype(matrix.dtype)
            mixed = jnp.where(live_cols[None, :, None], fresh, jnp.where(is_column[None, :, None], left[:, None, :], old))
            return jnp.where(live, mixed, old)

        work = lax.map(update, (work, multipliers, live_rows))
    return work.reshape(RB_DEV, NB * N_PROW, CB_DEV, NB * N_PCOL)
```

```python
import jax
import jax.numpy as jnp
from jax import lax
from jax.sharding import PartitionSpec as P


def ring_order(chips):
    side = round(chips**0.5)
    if side * side != chips or side % 2:
        return list(range(chips))
    walk = []
    for i in range(side):
        cols = list(range(1, side))
        walk += [i * side + k for k in (cols if i % 2 == 0 else cols[::-1])]
    return walk + [i * side for i in range(side - 1, -1, -1)]


def lookup(table, index):
    total = jnp.int32(0)
    for i, value in enumerate(table):
        total = jnp.where(index == i, jnp.int32(value), total)
    return total


def local(matrix, pattern, inverses, pivots):
    n = lax.axis_size("prow")
    m = lax.axis_size("pcol")
    r = lax.axis_index("prow")
    j = lax.axis_index("pcol")
    rb, width = matrix.shape[0], matrix.shape[1]
    half = width // 2
    chips = m // 2
    chip, core = j // 2, j % 2
    dt = matrix.dtype

    low_first = pivots[0, 1] == 0
    a_low = jnp.where(low_first, pivots[0, 0], pivots[1, 0])
    a_high = jnp.where(low_first, pivots[1, 0], pivots[0, 0])
    c0, c1 = pivots[0, 2], pivots[1, 2]
    is_low, is_high = r == n // 2, r == n // 2 - 1
    is_end = (r == 0) | (r == n - 1)
    out = jnp.where(
        r == 0, 0, jnp.where(is_low, a_low // n, jnp.where(is_high, a_high // n, rb - 1))
    )
    slots = [(out + 1 + k) % rb for k in range(rb)]

    blocks = matrix.reshape(rb, width, width)
    mine = lax.dynamic_slice(pattern.reshape(rb, n, m), (0, r, j), (rb, 1, 1)).reshape(rb)

    def block(slot):
        keep = lax.dynamic_index_in_dim(mine, slot, 0, keepdims=False) != 0
        one = lax.dynamic_index_in_dim(blocks, slot, 0, keepdims=False)
        return jnp.where(keep, one, jnp.zeros_like(one))

    raw = [block(s) for s in slots]
    leaving = raw[-1]

    def along(pairs, value):
        return lax.ppermute(value, "prow", pairs)

    first_hop = [(0, 1), (n - 1, n - 2), (n // 2, 0), (n // 2 - 1, n - 1)]
    za = along(first_hop, leaving)
    low = jnp.where(r == 0, leaving, za)
    high = jnp.where(r == n - 1, leaving, za)
    parts_low, parts_high = [], []
    for p in range(2):
        cut = slice(p * half, (p + 1) * half)
        got = za[cut]
        lo, hi = low[cut], high[cut]
        for h in range(1, n - 1):
            got = along([(h, h + 1), (n - 1 - h, n - 2 - h)], got)
            lo = jnp.where(r == h + 1, got, lo)
            hi = jnp.where(r == n - 2 - h, got, hi)
        parts_low.append(lo)
        parts_high.append(hi)
    row_low = jnp.concatenate(parts_low)
    row_high = jnp.concatenate(parts_high)
    upper = jnp.where(low_first, row_low, row_high)
    later = jnp.where(low_first, row_high, row_low)

    swap = [(i, i ^ 1) for i in range(m)]

    def sibling(value):
        return lax.ppermute(value, "pcol", swap)

    def own_half(value):
        return lax.dynamic_slice_in_dim(value, core * half, half, value.ndim - 2)

    def other_half(value):
        return lax.dynamic_slice_in_dim(value, (1 - core) * half, half, value.ndim - 2)

    def whole(own, other):
        top = jnp.where(core == 0, own, other)
        low_part = jnp.where(core == 0, other, own)
        return jnp.concatenate([top, low_part], axis=-2)

    order = ring_order(chips)
    place = [order.index(k) for k in range(chips)]
    around = []
    for i in range(chips):
        around.append((2 * order[i], 2 * order[(i + 1) % chips]))
        around.append((2 * order[i] + 1, 2 * order[(i - 1) % chips] + 1))

    def distance(column):
        gap = lookup(place, chip) - lookup(place, column // 2)
        return jnp.where(core == 0, gap, -gap) % chips

    early = jnp.stack(raw)
    early_own = own_half(early)
    early_sib = sibling(other_half(early))
    in_own = own_half(za)
    in_sib = sibling(other_half(za))

    def held(column, k):
        hit = column % 2 == core
        if k < rb - 1:
            return jnp.where(hit, early_own[k], early_sib[k])
        own = jnp.where(is_end, in_own, early_own[k])
        sib = jnp.where(is_end, in_sib, early_sib[k])
        return jnp.where(hit, own, sib)

    column_x = jnp.where((r == 0) == low_first, c1, c0)
    dist_x = distance(column_x)
    x = jnp.where(column_x % 2 == core, early_own[-1], early_sib[-1])
    for hop in range(chips - 1):
        got = lax.ppermute(x, "pcol", around)
        x = jnp.where(dist_x == hop + 1, got, x)
    x_low, x_high = x, x
    stride = n // 2
    while stride:
        pairs = []
        for i in range(0, n, 2 * stride):
            pairs += [(i, i + stride), (n - 1 - i, n - 1 - i - stride)]
        send = jnp.where(r % (2 * stride) == 0, x_low, x_high)
        got = along(pairs, send)
        x_low = jnp.where(r % (2 * stride) == stride, got, x_low)
        x_high = jnp.where((n - 1 - r) % (2 * stride) == stride, got, x_high)
        stride //= 2
    v_half = jnp.where(low_first, x_low, x_high)
    l_half = jnp.where(low_first, x_high, x_low)

    def product(left, right):
        return jnp.dot(left, right, preferred_element_type=jnp.float32)

    l_half = product(l_half, inverses[0]).astype(dt)
    vl_half = jnp.stack([v_half, l_half])
    vl = whole(vl_half, sibling(vl_half))
    v, left_later = vl[0], vl[1]

    columns = [c0, c1]
    dists = [distance(c) for c in columns]
    got = None
    gots = []
    for t in range(rb + chips - 2):
        send = []
        for q in range(2):
            own = held(columns[q], min(t, rb - 1))
            send.append(own if t == 0 else jnp.where(dists[q] == 0, own, got[q]))
        got = lax.ppermute(jnp.stack(send), "pcol", around)
        gots.append(got)

    def panel(q, k):
        value = held(columns[q], k)
        for d in range(1, chips):
            value = jnp.where(dists[q] == d, gots[k + d - 1][q], value)
        return value

    lefts = []
    for k in range(rb):
        m0 = product(panel(0, k), inverses[0]).astype(dt)
        p1 = (panel(1, k).astype(jnp.float32) - product(m0, v)).astype(dt)
        m1 = product(p1, inverses[1]).astype(dt)
        mm = jnp.stack([m0, m1])
        lefts.append(whole(mm, sibling(mm)))

    next_upper = (later.astype(jnp.float32) - product(left_later, upper)).astype(dt)
    raw[-1] = jnp.where(is_end, za, leaving)
    done = []
    for k in range(rb):
        m0, m1 = lefts[k][0], lefts[k][1]
        w = (raw[k].astype(jnp.float32) - product(m0, upper)).astype(dt)
        w = (w.astype(jnp.float32) - product(m1, next_upper)).astype(dt)
        done.append(jnp.where(j == c0, m0, jnp.where(j == c1, m1, w)))
    pivot_first = (is_low & low_first) | (is_high & ~low_first)
    pivot_later = (is_low & ~low_first) | (is_high & low_first)
    frozen = jnp.where(j == c0, left_later, next_upper)
    done[-1] = jnp.where(pivot_first, upper, jnp.where(pivot_later, frozen, done[-1]))
    result = jnp.stack(done)
    result = jnp.stack(
        [
            lax.dynamic_index_in_dim(result, (slot - out - 1) % rb, 0, keepdims=False)
            for slot in range(rb)
        ]
    )
    return result.reshape(matrix.shape)


def solution(mesh):
    placed = (P(None, "prow", None, "pcol"), P(), P(), P())
    return jax.shard_map(
        local, mesh=mesh, in_specs=placed, out_specs=P(None, "prow", None, "pcol"), check_vma=False
    )
```

```python
import functools

import jax
import jax.numpy as jnp
from jax import lax
from jax.experimental import pallas as pl
from jax.experimental.pallas import tpu as pltpu
from jax.sharding import PartitionSpec as P

SMEM = pl.BlockSpec(memory_space=pltpu.SMEM)
VMEM = pl.BlockSpec(memory_space=pltpu.VMEM)
ANY = pl.BlockSpec(memory_space=pl.ANY)
GRANT = pltpu.CompilerParams(vmem_limit_bytes=24 * 2**20)


def facts(n, m, rb, pivots):
    f = {}
    r = f["r"] = lax.axis_index("prow").astype(jnp.int32)
    j = f["j"] = lax.axis_index("pcol").astype(jnp.int32)
    f["core"] = j & 1
    f["chip"] = j >> 1
    low_first = f["low_first"] = pivots[0, 1] == 0
    shift = n.bit_length() - 1
    a_low = jnp.where(low_first, pivots[0, 0], pivots[1, 0]) >> shift
    a_high = jnp.where(low_first, pivots[1, 0], pivots[0, 0]) >> shift
    f["c"] = [pivots[0, 2], pivots[1, 2]]
    is_low, is_high = r == n // 2, r == n // 2 - 1
    f["is_low"], f["is_high"] = is_low, is_high
    f["is_end"] = jnp.logical_or(r == 0, r == n - 1)
    out = jnp.where(is_low, a_low, jnp.where(is_high, a_high, jnp.where(r == 0, 0, rb - 1)))
    f["slots"] = []
    for k in range(rb):
        slot = out + (1 + k)
        f["slots"].append(jnp.where(slot >= rb, slot - rb, slot))
    f["cx"] = jnp.where((r == 0) == low_first, pivots[1, 2], pivots[0, 2])
    return f


def either(cond, out_ref, yes, no):
    @pl.when(cond)
    def _():
        out_ref[...] = yes()

    @pl.when(jnp.logical_not(cond))
    def _():
        out_ref[...] = no()


def rows(part, half):
    return pl.ds(pl.multiple_of(part * half, half), half)


def prepare(n, m, piv, pat, mat, raw, leaving, other):
    rb, width = mat.shape[0], mat.shape[1]
    f = facts(n, m, rb, piv)
    cut = rows(1 - f["core"], width // 2)
    for k in reversed(range(rb)):
        slot = f["slots"][k]
        keep = pat[slot * n + f["r"], f["j"]] != 0
        zero = lambda: jnp.zeros((width, width), mat.dtype)
        either(keep, raw.at[k], lambda: mat[slot], zero)
        if k == rb - 1:
            leaving[...] = raw[k]
        other[k] = raw[k, cut, :]


def pick(n, m, piv, raw, sib, panel, extra):
    rb, width = raw.shape[0], raw.shape[1]
    f = facts(n, m, rb, piv)
    cut = rows(f["core"], width // 2)
    for q in range(2):
        hit = (f["c"][q] & 1) == f["core"]
        for k in range(rb - 1):
            either(hit, panel.at[q, k], lambda: raw[k, cut, :], lambda: sib[k])
    hit = (f["cx"] & 1) == f["core"]
    either(hit, extra, lambda: raw[rb - 1, cut, :], lambda: sib[rb - 1])


def pick_third(n, m, piv, raw, sib, moved, sib_moved, panel):
    rb, width = raw.shape[0], raw.shape[1]
    f = facts(n, m, rb, piv)
    cut = rows(f["core"], width // 2)
    for q in range(2):
        hit = (f["c"][q] & 1) == f["core"]

        @pl.when(f["is_end"])
        def _():
            either(hit, panel.at[q], lambda: moved[cut, :], lambda: sib_moved[cut, :])

        @pl.when(jnp.logical_not(f["is_end"]))
        def _():
            either(hit, panel.at[q], lambda: raw[rb - 1, cut, :], lambda: sib[rb - 1])


def bit_of(f, column, stage, stages):
    apart = f["chip"] ^ (column >> 1)
    bit = jnp.where(f["core"] == 0, stage, stages - 1 - stage)
    return ((apart >> bit) & 1) == 1


def forward(n, m, stage, stages, piv, had, got, panel):
    f = facts(n, m, 2, piv)
    for q in range(2):
        take = bit_of(f, f["c"][q], stage, stages)
        either(take, panel.at[q], lambda: got[q], lambda: had[q])


def forward_extra(n, m, stage, stages, piv, had, got, extra):
    f = facts(n, m, 2, piv)
    take = bit_of(f, f["cx"], stage, stages)
    either(take, extra, lambda: got[...], lambda: had[...])


def hand_on(n, m, stride, had, got, extra):
    r = lax.axis_index("prow").astype(jnp.int32)
    low = (r & (2 * stride - 1)) == stride
    high = ((n - 1 - r) & (2 * stride - 1)) == stride
    either(jnp.logical_or(low, high), extra, lambda: got[...], lambda: had[...])


def dot(left, right):
    return jnp.dot(left, right, preferred_element_type=jnp.float32)


def settle_extra(n, m, piv, inv, *refs):
    had, out = refs[:-1], refs[-1]
    f = facts(n, m, 2, piv)
    r = f["r"]
    stages = len(had) - 1
    for which in range(2):
        place = r if which == 0 else n - 1 - r
        low_is_v = f["low_first"] if which == 0 else jnp.logical_not(f["low_first"])
        for s in range(stages + 1):
            if s == 0:
                here = place == 0
            else:
                here = (place & (2 * (n >> s) - 1)) == (n >> s)

            @pl.when(jnp.logical_and(here, low_is_v))
            def _():
                out[0] = had[s][...]

            @pl.when(jnp.logical_and(here, jnp.logical_not(low_is_v)))
            def _():
                out[1] = had[s][...]

    out[1] = dot(out[1], inv[0]).astype(out.dtype)


def multiply(n, m, stages, blocks, piv, inv, vl, sib_vl, had, got, out, v):
    f = facts(n, m, 2, piv)
    half = vl.shape[1]
    v[rows(f["core"], half), :] = vl[0]
    v[rows(1 - f["core"], half), :] = sib_vl[0]
    take = [bit_of(f, f["c"][q], stages - 1, stages) for q in range(2)]
    for q in range(2):
        either(take[q], out.at[q], lambda: got[q], lambda: had[q])
    for k in range(blocks):
        where = (lambda q: (q, k)) if blocks > 1 else (lambda q: (q,))
        m0 = dot(out[where(0)], inv[0]).astype(out.dtype)
        p1 = (out[where(1)].astype(jnp.float32) - dot(m0, v[...])).astype(out.dtype)
        out[where(0)] = m0
        out[where(1)] = dot(p1, inv[1]).astype(out.dtype)


def settle_rows(n, m, piv, vl, sib_vl, leaving, moved, *refs):
    hops, upper, lefts = refs[:-2], refs[-2], refs[-1]
    width = leaving.shape[0]
    half = width // 2
    f = facts(n, m, 2, piv)
    r = f["r"]
    for which in range(2):
        place = r if which == 0 else n - 1 - r
        slot = jnp.where(f["low_first"], which, 1 - which)
        for h in range(n):

            @pl.when(place == h)
            def _():
                if h == 0:
                    upper[slot] = leaving[...]
                elif h == 1:
                    upper[slot] = moved[...]
                else:
                    upper[slot, :half, :] = hops[2 * (h - 2)][...]
                    upper[slot, half:, :] = hops[2 * (h - 2) + 1][...]

    lefts[rows(f["core"], half), :] = vl[1]
    lefts[rows(1 - f["core"], half), :] = sib_vl[1]
    for p in range(2):
        cut = slice(p * half, (p + 1) * half)
        fresh = upper[1, cut, :].astype(jnp.float32) - dot(lefts[cut, :], upper[0])
        upper[1, cut, :] = fresh.astype(upper.dtype)


def update(f, upper, mine, sib, at, old, new):
    half = old.shape[0] // 2
    for p in range(2):
        part = jnp.where(f["core"] == p, 0, 1)
        cut = slice(p * half, (p + 1) * half)

        def left(q):
            return jnp.where(part == 0, mine[(q, *at)], sib[(q, *at)])

        m0, m1 = left(0), left(1)

        @pl.when(f["j"] == f["c"][0])
        def _():
            new[cut, :] = m0

        @pl.when(f["j"] == f["c"][1])
        def _():
            new[cut, :] = m1

        @pl.when(jnp.logical_and(f["j"] != f["c"][0], f["j"] != f["c"][1]))
        def _():
            w = (old[cut, :].astype(jnp.float32) - dot(m0, upper[0])).astype(new.dtype)
            w = w.astype(jnp.float32) - dot(m1, upper[1])
            new[cut, :] = w.astype(new.dtype)


def update_stays(n, m, piv, upper, mine, sib, raw, out, new, sems):
    rb = raw.shape[0]
    f = facts(n, m, rb, piv)
    copies = []
    for k in range(rb - 1):
        update(f, upper, mine, sib, (k,), raw.at[k], new.at[k])
        copies.append(pltpu.make_async_copy(new.at[k], out.at[f["slots"][k]], sems.at[k]))
        copies[-1].start()
    for copy in copies:
        copy.wait()


def update_third(n, m, piv, upper, lefts, mine, sib, raw, moved, so_far, out, old, new, sem):
    del so_far
    rb = raw.shape[0]
    f = facts(n, m, rb, piv)
    low_first = f["low_first"]
    first = jnp.where(low_first, f["is_low"], f["is_high"])
    second = jnp.where(low_first, f["is_high"], f["is_low"])

    @pl.when(first)
    def _():
        new[...] = upper[0]

    @pl.when(second)
    def _():
        either(f["j"] == f["c"][0], new, lambda: lefts[...], lambda: upper[1])

    @pl.when(jnp.logical_not(jnp.logical_or(first, second)))
    def _():
        either(f["is_end"], old, lambda: moved[...], lambda: raw[rb - 1])
        update(f, upper, mine, sib, (), old, new)

    copy = pltpu.make_async_copy(new, out.at[f["slots"][rb - 1]], sem)
    copy.start()
    copy.wait()


def local(matrix, pattern, inverses, pivots):
    n = lax.axis_size("prow")
    m = lax.axis_size("pcol")
    rb, width = matrix.shape[0], matrix.shape[1]
    half = width // 2
    chips = m // 2
    stages = chips.bit_length() - 1
    dt = matrix.dtype
    blocks = matrix.reshape(rb, width, width)

    def call(kernel, shapes, specs, *operands, scratch=(), aliases=None, products=0, place=VMEM):
        outs = [jax.ShapeDtypeStruct(s, dt) for s in shapes]
        moved = sum(a.size * a.dtype.itemsize for a in operands)
        result = pl.pallas_call(
            kernel,
            out_shape=outs,
            in_specs=[SMEM if s == "s" else VMEM for s in specs] + [VMEM] * (len(operands) - len(specs) - len(aliases or {}))
            + [place] * len(aliases or {}),
            out_specs=[place] * len(outs),
            scratch_shapes=[pltpu.VMEM(s, dt) if isinstance(s, tuple) else s for s in scratch],
            input_output_aliases=aliases or {},
            compiler_params=GRANT,
            cost_estimate=pl.CostEstimate(
                flops=int(products * 2 * width**3), bytes_accessed=moved, transcendentals=0
            ),
        )(*operands)
        return result if len(result) > 1 else result[0]

    bind = lambda kernel, *args: functools.partial(kernel, n, m, *args)

    def along(pairs, value):
        return lax.ppermute(value, "prow", pairs)

    def sibling(value):
        return lax.ppermute(value, "pcol", [(i, i ^ 1) for i in range(m)])

    def across(stage, value):
        pairs = []
        for i in range(m):
            bit = stage if i % 2 == 0 else stages - 1 - stage
            pairs.append((i, i ^ (2 << bit)))
        return lax.ppermute(value, "pcol", pairs)

    raw, leaving, other = call(
        bind(prepare),
        [(rb, width, width), (width, width), (rb, half, width)],
        "ss",
        pivots,
        pattern,
        blocks,
    )
    early = sibling(other)
    moved = along([(0, 1), (n - 1, n - 2), (n // 2, 0), (n // 2 - 1, n - 1)], leaving)

    panel, extra = call(
        bind(pick), [(2, rb - 1, half, width), (half, width)], "s", pivots, raw, early
    )
    for s in range(stages):
        got = across(s, extra)
        extra = call(bind(forward_extra, s, stages), [(half, width)], "s", pivots, extra, got)
    for s in range(stages):
        got = across(s, panel)
        if s < stages - 1:
            panel = call(bind(forward, s, stages), [panel.shape], "s", pivots, panel, got)
    stays = (panel, got)

    came = [extra]
    send = extra
    stride = n // 2
    while stride:
        pairs = []
        for i in range(0, n, 2 * stride):
            pairs += [(i, i + stride), (n - 1 - i, n - 1 - i - stride)]
        got = along(pairs, send)
        came.append(got)
        if stride > 1:
            send = call(bind(hand_on, stride), [(half, width)], "", send, got)
        stride //= 2
    vl = call(bind(settle_extra), [(2, half, width)], "s", pivots, inverses, *came, products=0.5)
    sib_vl = sibling(vl)

    hops = []
    parts = [moved[:half], moved[half:]]
    for h in range(1, n - 1):
        parts = [along([(h, h + 1), (n - 1 - h, n - 2 - h)], part) for part in parts]
        hops += parts

    sib_moved = sibling(moved)
    third = call(
        bind(pick_third), [(2, half, width)], "s", pivots, raw, early, moved, sib_moved
    )
    for s in range(stages):
        got = across(s, third)
        if s < stages - 1:
            third = call(bind(forward, s, stages), [third.shape], "s", pivots, third, got)

    square = (width, width)
    mine = call(
        bind(multiply, stages, rb - 1),
        [(2, rb - 1, half, width)],
        "s",
        pivots,
        inverses,
        vl,
        sib_vl,
        *stays,
        scratch=[square],
        products=3 * (rb - 1) / 2,
    )
    sib_mine = sibling(mine)
    mine_third = call(
        bind(multiply, stages, 1),
        [(2, half, width)],
        "s",
        pivots,
        inverses,
        vl,
        sib_vl,
        third,
        got,
        scratch=[square],
        products=1.5,
    )
    sib_third = sibling(mine_third)
    upper, lefts = call(
        bind(settle_rows),
        [(2, width, width), square],
        "s",
        pivots,
        vl,
        sib_vl,
        leaving,
        moved,
        *hops,
        products=1,
    )
    result = call(
        bind(update_stays),
        [blocks.shape],
        "s",
        pivots,
        upper,
        mine,
        sib_mine,
        raw,
        scratch=[(rb - 1, width, width), pltpu.SemaphoreType.DMA((rb - 1,))],
        products=2 * (rb - 1),
        place=ANY,
    )
    result = call(
        bind(update_third),
        [blocks.shape],
        "s",
        pivots,
        upper,
        lefts,
        mine_third,
        sib_third,
        raw,
        moved,
        result,
        scratch=[square, square, pltpu.SemaphoreType.DMA],
        aliases={7: 0},
        products=2,
        place=ANY,
    )
    return result.reshape(matrix.shape)


def solution(mesh):
    placed = (P(None, "prow", None, "pcol"), P(), P(), P())
    return jax.shard_map(
        local, mesh=mesh, in_specs=placed, out_specs=P(None, "prow", None, "pcol"), check_vma=False
    )
```

```python
import functools

import jax
import jax.numpy as jnp
from jax import lax
from jax.experimental import pallas as pl
from jax.experimental.pallas import tpu as pltpu
from jax.sharding import PartitionSpec as P

SMEM = pl.BlockSpec(memory_space=pltpu.SMEM)
VMEM = pl.BlockSpec(memory_space=pltpu.VMEM)
ANY = pl.BlockSpec(memory_space=pl.ANY)
GRANT = pltpu.CompilerParams(vmem_limit_bytes=24 * 2**20)


def facts(n, m, rb, pivots):
    f = {}
    r = f["r"] = lax.axis_index("prow").astype(jnp.int32)
    j = f["j"] = lax.axis_index("pcol").astype(jnp.int32)
    f["core"] = j & 1
    f["chip"] = j >> 1
    low_first = f["low_first"] = pivots[0, 1] == 0
    shift = n.bit_length() - 1
    a_low = jnp.where(low_first, pivots[0, 0], pivots[1, 0]) >> shift
    a_high = jnp.where(low_first, pivots[1, 0], pivots[0, 0]) >> shift
    f["c"] = [pivots[0, 2], pivots[1, 2]]
    is_low, is_high = r == n // 2, r == n // 2 - 1
    f["is_low"], f["is_high"] = is_low, is_high
    f["is_end"] = jnp.logical_or(r == 0, r == n - 1)
    out = jnp.where(is_low, a_low, jnp.where(is_high, a_high, jnp.where(r == 0, 0, rb - 1)))
    f["slots"] = []
    for k in range(rb):
        slot = out + (1 + k)
        f["slots"].append(jnp.where(slot >= rb, slot - rb, slot))
    f["fixed_step"] = jnp.where(pivots[0, 2] == m - 1, 0, 1)
    f["free"] = pivots[0, 2] + pivots[1, 2] - (m - 1)
    f["cx"] = jnp.where((r == 0) == low_first, pivots[1, 2], pivots[0, 2])
    return f


def either(cond, out_ref, yes, no):
    @pl.when(cond)
    def _():
        out_ref[...] = yes()

    @pl.when(jnp.logical_not(cond))
    def _():
        out_ref[...] = no()


def rows(part, half):
    return pl.ds(pl.multiple_of(part * half, half), half)


def prepare(n, m, piv, pat, mat, raw, leaving, other):
    rb, width = mat.shape[0], mat.shape[1]
    f = facts(n, m, rb, piv)
    cut = rows(1 - f["core"], width // 2)
    for k in reversed(range(rb)):
        slot = f["slots"][k]
        keep = pat[f["j"], slot * n + f["r"]] != 0
        zero = lambda: jnp.zeros((width, width), mat.dtype)
        either(keep, raw.at[k], lambda: mat[slot], zero)
        if k == rb - 1:
            leaving[...] = raw[k]
        other[k] = raw[k, cut, :]


def pick_extra(n, m, piv, raw, sib, extra):
    rb, width = raw.shape[0], raw.shape[1]
    f = facts(n, m, rb, piv)
    cut = rows(f["core"], width // 2)
    hit = (f["cx"] & 1) == f["core"]
    either(hit, extra, lambda: raw[rb - 1, cut, :], lambda: sib[rb - 1])


def pick(n, m, piv, raw, sib, fixed, free):
    rb, width = raw.shape[0], raw.shape[1]
    f = facts(n, m, rb, piv)
    cut = rows(f["core"], width // 2)
    for panel, column in ((fixed, m - 1), (free, f["free"])):
        hit = (column & 1) == f["core"]
        for k in range(rb - 1):
            either(hit, panel.at[k], lambda: raw[k, cut, :], lambda: sib[k])


def pick_third(n, m, piv, raw, sib, moved, sib_moved, fixed, free):
    rb, width = raw.shape[0], raw.shape[1]
    f = facts(n, m, rb, piv)
    cut = rows(f["core"], width // 2)
    for panel, column in ((fixed, m - 1), (free, f["free"])):
        hit = (column & 1) == f["core"]

        @pl.when(f["is_end"])
        def _():
            either(hit, panel.at[0], lambda: moved[cut, :], lambda: sib_moved[cut, :])

        @pl.when(jnp.logical_not(f["is_end"]))
        def _():
            either(hit, panel.at[0], lambda: raw[rb - 1, cut, :], lambda: sib[rb - 1])


def bit_of(f, column, stage, stages):
    apart = f["chip"] ^ (column >> 1)
    bit = jnp.where(f["core"] == 0, stage, stages - 1 - stage)
    return ((apart >> bit) & 1) == 1


def forward(n, m, key, stage, stages, piv, had, got, out):
    f = facts(n, m, 2, piv)
    take = bit_of(f, f[key], stage, stages)
    either(take, out, lambda: got[...], lambda: had[...])


def ring_order(chips):
    side = round(chips**0.5)
    if side * side != chips or side % 2:
        return list(range(chips))
    walk = []
    for i in range(side):
        across = list(range(1, side))
        walk += [i * side + k for k in (across if i % 2 == 0 else across[::-1])]
    return walk + [i * side for i in range(side - 1, -1, -1)]


def ring_hops(chips):
    order = ring_order(chips)
    start = order.index(chips - 1)
    one = [order[(start + k) % chips] for k in range(chips)]
    two = [order[(start - k) % chips] for k in range(chips)]
    hops = [
        [(2 * one[h], 2 * one[h + 1]), (2 * two[h] + 1, 2 * two[h + 1] + 1)]
        for h in range(chips - 1)
    ]
    return one, two, hops


def hand_on(n, m, stride, had, got, extra):
    r = lax.axis_index("prow").astype(jnp.int32)
    low = (r & (2 * stride - 1)) == stride
    high = ((n - 1 - r) & (2 * stride - 1)) == stride
    either(jnp.logical_or(low, high), extra, lambda: got[...], lambda: had[...])


def dot(left, right):
    return jnp.dot(left, right, preferred_element_type=jnp.float32)


def settle_extra(n, m, piv, inv, *refs):
    had, out = refs[:-1], refs[-1]
    f = facts(n, m, 2, piv)
    r = f["r"]
    stages = len(had) - 1
    for which in range(2):
        place = r if which == 0 else n - 1 - r
        low_is_v = f["low_first"] if which == 0 else jnp.logical_not(f["low_first"])
        for s in range(stages + 1):
            if s == 0:
                here = place == 0
            else:
                here = (place & (2 * (n >> s) - 1)) == (n >> s)

            @pl.when(jnp.logical_and(here, low_is_v))
            def _():
                out[0] = had[s][...]

            @pl.when(jnp.logical_and(here, jnp.logical_not(low_is_v)))
            def _():
                out[1] = had[s][...]

    out[1] = dot(out[1], inv[0]).astype(out.dtype)


def multiply(n, m, stages, piv, inv, vl, sib_vl, free, free_got, *refs):
    fixed, out, v = refs[:-2], refs[-2], refs[-1]
    f = facts(n, m, 2, piv)
    half = vl.shape[1]
    v[rows(f["core"], half), :] = vl[0]
    v[rows(1 - f["core"], half), :] = sib_vl[0]
    chips = m // 2
    one, two, _ = ring_hops(chips)
    hop = jnp.int32(0)
    for chip in range(chips):
        here = jnp.where(f["core"] == 0, one.index(chip), two.index(chip))
        hop = jnp.where(f["chip"] == chip, here, hop)
    for h in range(chips):

        @pl.when(hop == h)
        def _():
            out[f["fixed_step"]] = fixed[h][...]

    take = bit_of(f, f["free"], stages - 1, stages)
    either(take, out.at[1 - f["fixed_step"]], lambda: free_got[...], lambda: free[...])
    for k in range(free.shape[0]):
        m0 = dot(out[0, k], inv[0]).astype(out.dtype)
        p1 = (out[1, k].astype(jnp.float32) - dot(m0, v[...])).astype(out.dtype)
        out[0, k] = m0
        out[1, k] = dot(p1, inv[1]).astype(out.dtype)


def settle_rows(n, m, piv, vl, sib_vl, leaving, moved, *refs):
    hops, upper, lefts = refs[:-2], refs[-2], refs[-1]
    width = leaving.shape[0]
    half = width // 2
    f = facts(n, m, 2, piv)
    r = f["r"]
    for which in range(2):
        place = r if which == 0 else n - 1 - r
        slot = jnp.where(f["low_first"], which, 1 - which)
        for h in range(n):

            @pl.when(place == h)
            def _():
                if h == 0:
                    upper[slot] = leaving[...]
                elif h == 1:
                    upper[slot] = moved[...]
                else:
                    upper[slot, :half, :] = hops[2 * (h - 2)][...]
                    upper[slot, half:, :] = hops[2 * (h - 2) + 1][...]

    lefts[rows(f["core"], half), :] = vl[1]
    lefts[rows(1 - f["core"], half), :] = sib_vl[1]
    for p in range(2):
        cut = slice(p * half, (p + 1) * half)
        fresh = upper[1, cut, :].astype(jnp.float32) - dot(lefts[cut, :], upper[0])
        upper[1, cut, :] = fresh.astype(upper.dtype)


def update(f, upper, mine, sib, at, old, new):
    half = old.shape[0] // 2
    for p in range(2):
        part = jnp.where(f["core"] == p, 0, 1)
        cut = slice(p * half, (p + 1) * half)

        def left(q):
            return jnp.where(part == 0, mine[(q, *at)], sib[(q, *at)])

        m0, m1 = left(0), left(1)

        @pl.when(f["j"] == f["c"][0])
        def _():
            new[cut, :] = m0

        @pl.when(f["j"] == f["c"][1])
        def _():
            new[cut, :] = m1

        @pl.when(jnp.logical_and(f["j"] != f["c"][0], f["j"] != f["c"][1]))
        def _():
            w = (old[cut, :].astype(jnp.float32) - dot(m0, upper[0])).astype(new.dtype)
            w = w.astype(jnp.float32) - dot(m1, upper[1])
            new[cut, :] = w.astype(new.dtype)


def update_stays(n, m, piv, upper, mine, sib, raw, out, new, sems):
    rb = raw.shape[0]
    f = facts(n, m, rb, piv)
    copies = []
    for k in range(rb - 1):
        update(f, upper, mine, sib, (k,), raw.at[k], new.at[k])
        copies.append(pltpu.make_async_copy(new.at[k], out.at[f["slots"][k]], sems.at[k]))
        copies[-1].start()
    for copy in copies:
        copy.wait()


def update_third(n, m, piv, upper, lefts, mine, sib, raw, moved, so_far, out, old, new, sem):
    del so_far
    rb = raw.shape[0]
    f = facts(n, m, rb, piv)
    low_first = f["low_first"]
    first = jnp.where(low_first, f["is_low"], f["is_high"])
    second = jnp.where(low_first, f["is_high"], f["is_low"])

    @pl.when(first)
    def _():
        new[...] = upper[0]

    @pl.when(second)
    def _():
        either(f["j"] == f["c"][0], new, lambda: lefts[...], lambda: upper[1])

    @pl.when(jnp.logical_not(jnp.logical_or(first, second)))
    def _():
        either(f["is_end"], old, lambda: moved[...], lambda: raw[rb - 1])
        update(f, upper, mine, sib, (0,), old, new)

    copy = pltpu.make_async_copy(new, out.at[f["slots"][rb - 1]], sem)
    copy.start()
    copy.wait()


def local(matrix, pattern, inverses, pivots):
    n = lax.axis_size("prow")
    m = lax.axis_size("pcol")
    rb, width = matrix.shape[0], matrix.shape[1]
    half = width // 2
    chips = m // 2
    stages = chips.bit_length() - 1
    dt = matrix.dtype
    blocks = matrix.reshape(rb, width, width)

    def call(kernel, shapes, specs, *operands, scratch=(), aliases=(), products=0, place=VMEM, after=(), name=None):
        outs = [jax.ShapeDtypeStruct(s, dt) for s in shapes]
        count = len(operands)
        scratch = [pltpu.VMEM(s, dt) if isinstance(s, tuple) else s for s in scratch]

        def body(*refs):
            kernel(n, m, *refs[:count], *refs[count + len(after) :])

        kinds = {"s": SMEM, "v": VMEM, "a": ANY}
        specs = [kinds[k] for k in specs.ljust(count, "v")] + [ANY] * len(after)
        result = pl.pallas_call(
            body,
            out_shape=outs,
            in_specs=specs,
            out_specs=[place] * len(outs),
            scratch_shapes=scratch,
            input_output_aliases=dict(aliases),
            compiler_params=GRANT,
            name=name or kernel.__name__,
            cost_estimate=pl.CostEstimate(
                flops=int(products * 2 * width**3),
                bytes_accessed=sum(a.size * a.dtype.itemsize for a in operands),
                transcendentals=0,
            ),
        )(*operands, *after)
        return result if len(result) > 1 else result[0]

    def along(name, pairs, value):
        with jax.named_scope(name):
            return lax.ppermute(value, "prow", pairs)

    def sibling(name, value):
        with jax.named_scope(name):
            return lax.ppermute(value, "pcol", [(i, i ^ 1) for i in range(m)])

    def across(name, stage, value):
        pairs = []
        for i in range(m):
            bit = stage if i % 2 == 0 else stages - 1 - stage
            pairs.append((i, i ^ (2 << bit)))
        with jax.named_scope(name):
            return lax.ppermute(value, "pcol", pairs)

    def ring(name, value):
        came = [value]
        for h, pairs in enumerate(ring_hops(chips)[2]):
            with jax.named_scope(name + str(h)):
                came.append(lax.ppermute(came[-1], "pcol", pairs))
        return came

    def passing(name, key, value, after=()):
        for s in range(stages):
            got = across(name + str(s), s, value)
            if s < stages - 1:
                kernel = functools.partial(forward, n, m, key, s, stages)
                step = lambda _n, _m, *refs: kernel(*refs)
                value = call(step, [value.shape], "s", pivots, value, got, after=after, name="forward_" + name)
        return value, got

    square, strip = (width, width), (half, width)
    raw, leaving, other = call(
        prepare,
        [(rb, *square), square, (rb, *strip)],
        "ss",
        pivots,
        pattern.T,
        blocks,
    )
    moved = along("swap", [(0, 1), (n - 1, n - 2), (n // 2, 0), (n // 2 - 1, n - 1)], leaving)
    early = sibling("sib_early", other)

    extra = call(pick_extra, [strip], "s", pivots, raw, early)
    had, got = passing("extra", "cx", extra)
    step = lambda _n, _m, *refs: forward(n, m, "cx", stages - 1, stages, *refs)
    extra_here = call(step, [strip], "s", pivots, had, got, after=[moved], name="extra_here")
    fixed, free = call(
        pick, [(rb - 1, *strip)] * 2, "s", pivots, raw, early, after=[extra]
    )
    free_stays = passing("free", "free", free)
    fixed_stays = ring("fixed", fixed)

    hops = []
    parts = [moved[:half], moved[half:]]
    for h in range(1, n - 1):
        pairs = [(h, h + 1), (n - 1 - h, n - 2 - h)]
        parts = [along("row" + str(h), pairs, part) for part in parts]
        hops += parts

    sib_moved = sibling("sib_moved", moved)
    fixed, free = call(
        pick_third, [(1, *strip)] * 2, "s", pivots, raw, early, moved, sib_moved
    )

    came = [extra_here]
    send = extra_here
    stride = n // 2
    while stride:
        pairs = []
        for i in range(0, n, 2 * stride):
            pairs += [(i, i + stride), (n - 1 - i, n - 1 - i - stride)]
        got = along("extra_z", pairs, send)
        came.append(got)
        if stride > 1:
            step = lambda _n, _m, *refs: hand_on(n, m, stride, *refs)
            send = call(step, [strip], "", send, got, name="hand_on", after=[free])
        stride //= 2
    vl = call(settle_extra, [(2, *strip)], "s", pivots, inverses, *came, products=0.5, after=hops[:2])
    sib_vl = sibling("sib_vl", vl)

    free_third = passing("free_third", "free", free)
    fixed_third = ring("fixed_third", fixed)

    step = lambda _n, _m, *refs: multiply(n, m, stages, *refs)
    mine = call(
        step,
        [(2, rb - 1, *strip)],
        "s",
        pivots,
        inverses,
        vl,
        sib_vl,
        *free_stays,
        *fixed_stays,
        scratch=[square],
        products=3 * (rb - 1) / 2,
        name="multiply_stays",
    )
    sib_mine = sibling("sib_mine", mine)
    upper, lefts = call(
        settle_rows,
        [(2, *square), square],
        "s",
        pivots,
        vl,
        sib_vl,
        leaving,
        moved,
        *hops,
        products=1,
    )
    mine_third = call(
        step,
        [(2, 1, *strip)],
        "s",
        pivots,
        inverses,
        vl,
        sib_vl,
        *free_third,
        *fixed_third,
        scratch=[square],
        products=1.5,
        after=[upper],
        name="multiply_third",
    )
    sib_third = sibling("sib_third", mine_third)
    result = call(
        update_stays,
        [blocks.shape],
        "s",
        pivots,
        upper,
        mine,
        sib_mine,
        raw,
        scratch=[(rb - 1, *square), pltpu.SemaphoreType.DMA((rb - 1,))],
        products=2 * (rb - 1),
        place=ANY,
    )
    result = call(
        update_third,
        [blocks.shape],
        "svvvvvva",
        pivots,
        upper,
        lefts,
        mine_third,
        sib_third,
        raw,
        moved,
        result,
        scratch=[square, square, pltpu.SemaphoreType.DMA],
        aliases={7: 0},
        products=2,
        place=ANY,
    )
    return result.reshape(matrix.shape)


def solution(mesh):
    placed = (P(None, "prow", None, "pcol"), P(), P(), P())
    return jax.shard_map(
        local, mesh=mesh, in_specs=placed, out_specs=P(None, "prow", None, "pcol"), check_vma=False
    )
```

```python
import functools

import jax
import jax.numpy as jnp
from jax import lax
from jax.experimental import pallas as pl
from jax.experimental.pallas import tpu as pltpu
from jax.sharding import PartitionSpec as P

SMEM = pl.BlockSpec(memory_space=pltpu.SMEM)
VMEM = pl.BlockSpec(memory_space=pltpu.VMEM)
ANY = pl.BlockSpec(memory_space=pl.ANY)
GRANT = pltpu.CompilerParams(vmem_limit_bytes=24 * 2**20)


def facts(n, m, rb, pivots):
    f = {}
    r = f["r"] = lax.axis_index("prow").astype(jnp.int32)
    j = f["j"] = lax.axis_index("pcol").astype(jnp.int32)
    f["core"] = j & 1
    f["chip"] = j >> 1
    low_first = f["low_first"] = pivots[0, 1] == 0
    shift = n.bit_length() - 1
    a_low = jnp.where(low_first, pivots[0, 0], pivots[1, 0]) >> shift
    a_high = jnp.where(low_first, pivots[1, 0], pivots[0, 0]) >> shift
    f["c"] = [pivots[0, 2], pivots[1, 2]]
    is_low, is_high = r == n // 2, r == n // 2 - 1
    f["is_low"], f["is_high"] = is_low, is_high
    f["is_end"] = jnp.logical_or(r == 0, r == n - 1)
    out = jnp.where(is_low, a_low, jnp.where(is_high, a_high, jnp.where(r == 0, 0, rb - 1)))
    f["slots"] = []
    for k in range(rb):
        slot = out + (1 + k)
        f["slots"].append(jnp.where(slot >= rb, slot - rb, slot))
    f["fixed_step"] = jnp.where(pivots[0, 2] == m - 1, 0, 1)
    f["free"] = pivots[0, 2] + pivots[1, 2] - (m - 1)
    f["cx"] = jnp.where((r == 0) == low_first, pivots[1, 2], pivots[0, 2])
    return f


def either(cond, out_ref, yes, no):
    @pl.when(cond)
    def _():
        out_ref[...] = yes()

    @pl.when(jnp.logical_not(cond))
    def _():
        out_ref[...] = no()


def rows(part, half):
    return pl.ds(pl.multiple_of(part * half, half), half)


def prepare(n, m, piv, pat, mat, raw, leaving, other):
    rb, width = mat.shape[0], mat.shape[1]
    f = facts(n, m, rb, piv)
    cut = rows(1 - f["core"], width // 2)
    for k in reversed(range(rb)):
        slot = f["slots"][k]
        keep = pat[f["j"], slot * n + f["r"]] != 0
        zero = lambda: jnp.zeros((width, width), mat.dtype)
        either(keep, raw.at[k], lambda: mat[slot], zero)
        if k == rb - 1:
            leaving[...] = raw[k]
        other[k] = raw[k, cut, :]


def pick_extra(n, m, piv, raw, sib, extra):
    rb, width = raw.shape[0], raw.shape[1]
    f = facts(n, m, rb, piv)
    cut = rows(f["core"], width // 2)
    hit = (f["cx"] & 1) == f["core"]
    either(hit, extra, lambda: raw[rb - 1, cut, :], lambda: sib[rb - 1])


def pick(n, m, piv, raw, sib, fixed, free):
    rb, width = raw.shape[0], raw.shape[1]
    f = facts(n, m, rb, piv)
    cut = rows(f["core"], width // 2)
    for panel, column in ((fixed, m - 1), (free, f["free"])):
        hit = (column & 1) == f["core"]
        for k in range(rb - 1):
            either(hit, panel.at[k], lambda: raw[k, cut, :], lambda: sib[k])


def pick_third(n, m, piv, raw, sib, moved, sib_moved, fixed, free):
    rb, width = raw.shape[0], raw.shape[1]
    f = facts(n, m, rb, piv)
    cut = rows(f["core"], width // 2)
    for panel, column in ((fixed, m - 1), (free, f["free"])):
        hit = (column & 1) == f["core"]

        @pl.when(f["is_end"])
        def _():
            either(hit, panel.at[0], lambda: moved[cut, :], lambda: sib_moved[cut, :])

        @pl.when(jnp.logical_not(f["is_end"]))
        def _():
            either(hit, panel.at[0], lambda: raw[rb - 1, cut, :], lambda: sib[rb - 1])


def bit_of(f, column, stage, stages):
    apart = f["chip"] ^ (column >> 1)
    bit = jnp.where(f["core"] == 0, stage, stages - 1 - stage)
    return ((apart >> bit) & 1) == 1


def forward(n, m, key, stage, stages, piv, had, got, out):
    f = facts(n, m, 2, piv)
    take = bit_of(f, f[key], stage, stages)
    either(take, out, lambda: got[...], lambda: had[...])


def forward_both(n, m, key, stage, stages, piv, had, got, moved, out, moved_out):
    forward(n, m, key, stage, stages, piv, had, got, out)
    moved_out[...] = moved[...]


def ring_order(chips):
    side = round(chips**0.5)
    if side * side != chips or side % 2:
        return list(range(chips))
    walk = []
    for i in range(side):
        across = list(range(1, side))
        walk += [i * side + k for k in (across if i % 2 == 0 else across[::-1])]
    return walk + [i * side for i in range(side - 1, -1, -1)]


def ring_hops(chips):
    order = ring_order(chips)
    start = order.index(chips - 1)
    one = [order[(start + k) % chips] for k in range(chips)]
    two = [order[(start - k) % chips] for k in range(chips)]
    hops = [
        [(2 * one[h], 2 * one[h + 1]), (2 * two[h] + 1, 2 * two[h + 1] + 1)]
        for h in range(chips - 1)
    ]
    return one, two, hops


def hand_on(n, m, stride, had, got, extra):
    r = lax.axis_index("prow").astype(jnp.int32)
    low = (r & (2 * stride - 1)) == stride
    high = ((n - 1 - r) & (2 * stride - 1)) == stride
    either(jnp.logical_or(low, high), extra, lambda: got[...], lambda: had[...])


def dot(left, right):
    return jnp.dot(left, right, preferred_element_type=jnp.float32)


def settle_extra(n, m, piv, inv, *refs):
    had, out = refs[:-1], refs[-1]
    f = facts(n, m, 2, piv)
    r = f["r"]
    stages = len(had) - 1
    for which in range(2):
        place = r if which == 0 else n - 1 - r
        low_is_v = f["low_first"] if which == 0 else jnp.logical_not(f["low_first"])
        for s in range(stages + 1):
            if s == 0:
                here = place == 0
            else:
                here = (place & (2 * (n >> s) - 1)) == (n >> s)

            @pl.when(jnp.logical_and(here, low_is_v))
            def _():
                out[0] = had[s][...]

            @pl.when(jnp.logical_and(here, jnp.logical_not(low_is_v)))
            def _():
                out[1] = had[s][...]

    out[1] = dot(out[1], inv[0]).astype(out.dtype)


def multiply(n, m, stages, piv, inv, vl, sib_vl, free, free_got, *refs):
    fixed, out, v = refs[:-2], refs[-2], refs[-1]
    f = facts(n, m, 2, piv)
    half = vl.shape[1]
    v[rows(f["core"], half), :] = vl[0]
    v[rows(1 - f["core"], half), :] = sib_vl[0]
    chips = m // 2
    one, two, _ = ring_hops(chips)
    hop = jnp.int32(0)
    for chip in range(chips):
        here = jnp.where(f["core"] == 0, one.index(chip), two.index(chip))
        hop = jnp.where(f["chip"] == chip, here, hop)
    for h in range(chips):

        @pl.when(hop == h)
        def _():
            out[f["fixed_step"]] = fixed[h][...]

    take = bit_of(f, f["free"], stages - 1, stages)
    either(take, out.at[1 - f["fixed_step"]], lambda: free_got[...], lambda: free[...])
    for k in range(free.shape[0]):
        m0 = dot(out[0, k], inv[0]).astype(out.dtype)
        p1 = (out[1, k].astype(jnp.float32) - dot(m0, v[...])).astype(out.dtype)
        out[0, k] = m0
        out[1, k] = dot(p1, inv[1]).astype(out.dtype)


def settle_rows(n, m, piv, vl, sib_vl, leaving, moved, *refs):
    hops, upper, lefts = refs[:-2], refs[-2], refs[-1]
    width = leaving.shape[0]
    half = width // 2
    f = facts(n, m, 2, piv)
    r = f["r"]
    for which in range(2):
        place = r if which == 0 else n - 1 - r
        slot = jnp.where(f["low_first"], which, 1 - which)
        for h in range(n):

            @pl.when(place == h)
            def _():
                if h == 0:
                    upper[slot] = leaving[...]
                elif h == 1:
                    upper[slot] = moved[...]
                else:
                    upper[slot, :half, :] = hops[2 * (h - 2)][...]
                    upper[slot, half:, :] = hops[2 * (h - 2) + 1][...]

    lefts[rows(f["core"], half), :] = vl[1]
    lefts[rows(1 - f["core"], half), :] = sib_vl[1]
    for p in range(2):
        cut = slice(p * half, (p + 1) * half)
        fresh = upper[1, cut, :].astype(jnp.float32) - dot(lefts[cut, :], upper[0])
        upper[1, cut, :] = fresh.astype(upper.dtype)


def update(f, upper, mine, sib, at, old, new):
    half = old.shape[0] // 2
    for p in range(2):
        part = jnp.where(f["core"] == p, 0, 1)
        cut = slice(p * half, (p + 1) * half)

        def left(q):
            return jnp.where(part == 0, mine[(q, *at)], sib[(q, *at)])

        m0, m1 = left(0), left(1)

        @pl.when(f["j"] == f["c"][0])
        def _():
            new[cut, :] = m0

        @pl.when(f["j"] == f["c"][1])
        def _():
            new[cut, :] = m1

        @pl.when(jnp.logical_and(f["j"] != f["c"][0], f["j"] != f["c"][1]))
        def _():
            w = (old[cut, :].astype(jnp.float32) - dot(m0, upper[0])).astype(new.dtype)
            w = w.astype(jnp.float32) - dot(m1, upper[1])
            new[cut, :] = w.astype(new.dtype)


def update_stays(n, m, piv, upper, mine, sib, raw, out, new, sems):
    rb = raw.shape[0]
    f = facts(n, m, rb, piv)
    copies = []
    for k in range(rb - 1):
        update(f, upper, mine, sib, (k,), raw.at[k], new.at[k])
        copies.append(pltpu.make_async_copy(new.at[k], out.at[f["slots"][k]], sems.at[k]))
        copies[-1].start()
    for copy in copies:
        copy.wait()


def update_third(n, m, piv, upper, lefts, mine, sib, raw, moved, so_far, out, old, new, sem):
    del so_far
    rb = raw.shape[0]
    f = facts(n, m, rb, piv)
    low_first = f["low_first"]
    first = jnp.where(low_first, f["is_low"], f["is_high"])
    second = jnp.where(low_first, f["is_high"], f["is_low"])

    @pl.when(first)
    def _():
        new[...] = upper[0]

    @pl.when(second)
    def _():
        either(f["j"] == f["c"][0], new, lambda: lefts[...], lambda: upper[1])

    @pl.when(jnp.logical_not(jnp.logical_or(first, second)))
    def _():
        either(f["is_end"], old, lambda: moved[...], lambda: raw[rb - 1])
        update(f, upper, mine, sib, (0,), old, new)

    copy = pltpu.make_async_copy(new, out.at[f["slots"][rb - 1]], sem)
    copy.start()
    copy.wait()


def local(matrix, pattern, inverses, pivots):
    n = lax.axis_size("prow")
    m = lax.axis_size("pcol")
    rb, width = matrix.shape[0], matrix.shape[1]
    half = width // 2
    chips = m // 2
    stages = chips.bit_length() - 1
    dt = matrix.dtype
    blocks = matrix.reshape(rb, width, width)

    def call(kernel, shapes, specs, *operands, scratch=(), aliases=(), products=0, place=VMEM, after=(), name=None, weight=0):
        outs = [jax.ShapeDtypeStruct(s, dt) for s in shapes]
        count = len(operands)
        scratch = [pltpu.VMEM(s, dt) if isinstance(s, tuple) else s for s in scratch]

        def body(*refs):
            kernel(n, m, *refs[:count], *refs[count + len(after) :])

        kinds = {"s": SMEM, "v": VMEM, "a": ANY}
        specs = [kinds[k] for k in specs.ljust(count, "v")] + [ANY] * len(after)
        result = pl.pallas_call(
            body,
            out_shape=outs,
            in_specs=specs,
            out_specs=[place] * len(outs),
            scratch_shapes=scratch,
            input_output_aliases=dict(aliases),
            compiler_params=GRANT,
            name=name or kernel.__name__,
            cost_estimate=pl.CostEstimate(
                flops=int(products * 2 * width**3),
                bytes_accessed=weight + sum(a.size * a.dtype.itemsize for a in operands),
                transcendentals=0,
            ),
        )(*operands, *after)
        return result if len(result) > 1 else result[0]

    def along(name, pairs, value):
        with jax.named_scope(name):
            return lax.ppermute(value, "prow", pairs)

    def sibling(name, value):
        with jax.named_scope(name):
            return lax.ppermute(value, "pcol", [(i, i ^ 1) for i in range(m)])

    def across(name, stage, value):
        pairs = []
        for i in range(m):
            bit = stage if i % 2 == 0 else stages - 1 - stage
            pairs.append((i, i ^ (2 << bit)))
        with jax.named_scope(name):
            return lax.ppermute(value, "pcol", pairs)

    def ring(name, value):
        came = [value]
        for h, pairs in enumerate(ring_hops(chips)[2]):
            with jax.named_scope(name + str(h)):
                came.append(lax.ppermute(came[-1], "pcol", pairs))
        return came

    def passing(name, key, value, after=(), weight=0):
        for s in range(stages):
            got = across(name + str(s), s, value)
            if s < stages - 1:
                kernel = functools.partial(forward, n, m, key, s, stages)
                step = lambda _n, _m, *refs: kernel(*refs)
                label = "forward_" + name
                value = call(
                    step, [value.shape], "s", pivots, value, got, after=after, name=label, weight=weight
                )
        return value, got

    square, strip = (width, width), (half, width)
    raw, leaving, other = call(
        prepare,
        [(rb, *square), square, (rb, *strip)],
        "ss",
        pivots,
        pattern.T,
        blocks,
    )
    moved = along("swap", [(0, 1), (n - 1, n - 2), (n // 2, 0), (n // 2 - 1, n - 1)], leaving)
    early = sibling("sib_early", other)

    extra = call(pick_extra, [strip], "s", pivots, raw, early)
    fixed, free = call(
        pick, [(rb - 1, *strip)] * 2, "s", pivots, raw, early, after=[extra]
    )
    had, got = passing("extra", "cx", extra, after=[fixed], weight=16 * 2**20)
    fixed_stays = ring("fixed", fixed)
    free_got = across("free0", 0, free)
    if stages > 1:
        step = lambda _n, _m, *refs: forward_both(n, m, "free", 0, stages, *refs)
        free, moved = call(
            step,
            [free.shape, square],
            "s",
            pivots,
            free,
            free_got,
            moved,
            after=[had, fixed_stays[1]],
            name="forward_free",
        )
        free_got = across("free1", 1, free)
    for s in range(2, stages):
        step = lambda _n, _m, *refs: forward(n, m, "free", s - 1, stages, *refs)
        free = call(step, [free.shape], "s", pivots, free, free_got, name="forward_free")
        free_got = across("free" + str(s), s, free)
    free_stays = free, free_got
    step = lambda _n, _m, *refs: forward(n, m, "cx", stages - 1, stages, *refs)
    extra_here = call(
        step, [strip], "s", pivots, had, got, after=[free], name="extra_here"
    )

    hops = []
    parts = [moved[:half], moved[half:]]
    for h in range(1, n - 1):
        pairs = [(h, h + 1), (n - 1 - h, n - 2 - h)]
        parts = [along("row" + str(h), pairs, part) for part in parts]
        hops += parts

    sib_moved = sibling("sib_moved", moved)
    fixed, free = call(
        pick_third,
        [(1, *strip)] * 2,
        "s",
        pivots,
        raw,
        early,
        moved,
        sib_moved,
        after=[extra_here],
    )
    fixed_third = ring("fixed_third", fixed)
    free_third = passing("free_third", "free", free, after=[fixed_stays[2], free_got])

    came = [extra_here]
    send = extra_here
    stride = n // 2
    while stride:
        pairs = []
        for i in range(0, n, 2 * stride):
            pairs += [(i, i + stride), (n - 1 - i, n - 1 - i - stride)]
        got = along("extra_z", pairs, send)
        came.append(got)
        if stride > 1:
            step = lambda _n, _m, *refs: hand_on(n, m, stride, *refs)
            send = call(
                step,
                [strip],
                "",
                send,
                got,
                name="hand_on",
                after=[hops[0], fixed_third[1], free_third[0]],
            )
        stride //= 2
    vl = call(
        settle_extra,
        [(2, *strip)],
        "s",
        pivots,
        inverses,
        *came,
        products=0.5,
        after=[hops[1], fixed_stays[3], fixed_third[2], free_third[1]],
    )
    sib_vl = sibling("sib_vl", vl)

    step = lambda _n, _m, *refs: multiply(n, m, stages, *refs)
    mine = call(
        step,
        [(2, rb - 1, *strip)],
        "s",
        pivots,
        inverses,
        vl,
        sib_vl,
        *free_stays,
        *fixed_stays,
        scratch=[square],
        products=3 * (rb - 1) / 2,
        name="multiply_stays",
        after=[fixed_third[-1], hops[2]],
    )
    sib_mine = sibling("sib_mine", mine)
    upper, lefts = call(
        settle_rows,
        [(2, *square), square],
        "s",
        pivots,
        vl,
        sib_vl,
        leaving,
        moved,
        *hops,
        products=1,
        after=[mine],
    )
    mine_third = call(
        step,
        [(2, 1, *strip)],
        "s",
        pivots,
        inverses,
        vl,
        sib_vl,
        *free_third,
        *fixed_third,
        scratch=[square],
        products=1.5,
        after=[upper],
        name="multiply_third",
    )
    sib_third = sibling("sib_third", mine_third)
    result = call(
        update_stays,
        [blocks.shape],
        "s",
        pivots,
        upper,
        mine,
        sib_mine,
        raw,
        scratch=[(rb - 1, *square), pltpu.SemaphoreType.DMA((rb - 1,))],
        products=2 * (rb - 1),
        place=ANY,
    )
    result = call(
        update_third,
        [blocks.shape],
        "svvvvvva",
        pivots,
        upper,
        lefts,
        mine_third,
        sib_third,
        raw,
        moved,
        result,
        scratch=[square, square, pltpu.SemaphoreType.DMA],
        aliases={7: 0},
        products=2,
        place=ANY,
    )
    return result.reshape(matrix.shape)


def solution(mesh):
    placed = (P(None, "prow", None, "pcol"), P(), P(), P())
    return jax.shard_map(
        local, mesh=mesh, in_specs=placed, out_specs=P(None, "prow", None, "pcol"), check_vma=False
    )
```

```python
import functools

import jax
import jax.numpy as jnp
from jax import lax
from jax.experimental import pallas as pl
from jax.experimental.pallas import tpu as pltpu
from jax.sharding import PartitionSpec as P

SMEM = pl.BlockSpec(memory_space=pltpu.SMEM)
VMEM = pl.BlockSpec(memory_space=pltpu.VMEM)
ANY = pl.BlockSpec(memory_space=pl.ANY)
GRANT = pltpu.CompilerParams(vmem_limit_bytes=24 * 2**20)


def facts(n, m, rb, pivots):
    f = {}
    r = f["r"] = lax.axis_index("prow").astype(jnp.int32)
    j = f["j"] = lax.axis_index("pcol").astype(jnp.int32)
    f["core"] = j & 1
    f["chip"] = j >> 1
    low_first = f["low_first"] = pivots[0, 1] == 0
    shift = n.bit_length() - 1
    a_low = jnp.where(low_first, pivots[0, 0], pivots[1, 0]) >> shift
    a_high = jnp.where(low_first, pivots[1, 0], pivots[0, 0]) >> shift
    f["c"] = [pivots[0, 2], pivots[1, 2]]
    is_low, is_high = r == n // 2, r == n // 2 - 1
    f["is_low"], f["is_high"] = is_low, is_high
    f["is_end"] = jnp.logical_or(r == 0, r == n - 1)
    out = jnp.where(is_low, a_low, jnp.where(is_high, a_high, jnp.where(r == 0, 0, rb - 1)))
    f["slots"] = []
    for k in range(rb):
        slot = out + (1 + k)
        f["slots"].append(jnp.where(slot >= rb, slot - rb, slot))
    f["cx"] = jnp.where((r == 0) == low_first, pivots[1, 2], pivots[0, 2])
    return f


def either(cond, out_ref, yes, no):
    @pl.when(cond)
    def _():
        out_ref[...] = yes()

    @pl.when(jnp.logical_not(cond))
    def _():
        out_ref[...] = no()


def rows(part, half):
    return pl.ds(pl.multiple_of(part * half, half), half)


def prepare(n, m, piv, pat, mat, raw, leaving, other):
    rb, width = mat.shape[0], mat.shape[1]
    f = facts(n, m, rb, piv)
    cut = rows(1 - f["core"], width // 2)
    for k in reversed(range(rb)):
        slot = f["slots"][k]
        keep = pat[f["j"], slot * n + f["r"]] != 0
        zero = lambda: jnp.zeros((width, width), mat.dtype)
        either(keep, raw.at[k], lambda: mat[slot], zero)
        if k == rb - 1:
            leaving[...] = raw[k]
        other[k] = raw[k, cut, :]


def pick_extra(n, m, piv, raw, sib, extra):
    rb, width = raw.shape[0], raw.shape[1]
    f = facts(n, m, rb, piv)
    cut = rows(f["core"], width // 2)
    hit = (f["cx"] & 1) == f["core"]
    either(hit, extra, lambda: raw[rb - 1, cut, :], lambda: sib[rb - 1])


def pair(refs):
    return [refs[0].at[q] for q in range(2)] if len(refs) == 1 else list(refs)


def pick(n, m, piv, raw, sib, *panel):
    rb, width = raw.shape[0], raw.shape[1]
    f = facts(n, m, rb, piv)
    cut = rows(f["core"], width // 2)
    for q in range(2):
        hit = (f["c"][q] & 1) == f["core"]
        for k in range(rb - 1):
            either(hit, pair(panel)[q].at[k], lambda: raw[k, cut, :], lambda: sib[k])


def pick_third(n, m, piv, raw, sib, moved, sib_moved, panel):
    rb, width = raw.shape[0], raw.shape[1]
    f = facts(n, m, rb, piv)
    cut = rows(f["core"], width // 2)
    for q in range(2):
        hit = (f["c"][q] & 1) == f["core"]

        @pl.when(f["is_end"])
        def _():
            either(hit, panel.at[q, 0], lambda: moved[cut, :], lambda: sib_moved[cut, :])

        @pl.when(jnp.logical_not(f["is_end"]))
        def _():
            either(hit, panel.at[q, 0], lambda: raw[rb - 1, cut, :], lambda: sib[rb - 1])


def relay(n, m, moved, out, *halves):
    out[...] = moved[...]
    half = moved.shape[0] // 2
    for p, ref in enumerate(halves):
        ref[...] = moved[p * half : (p + 1) * half, :]


def bit_of(f, column, stage, stages):
    apart = f["chip"] ^ (column >> 1)
    bit = jnp.where(f["core"] == 0, stage, stages - 1 - stage)
    return ((apart >> bit) & 1) == 1


def forward_extra(n, m, stage, stages, piv, had, got, out):
    f = facts(n, m, 2, piv)
    take = bit_of(f, f["cx"], stage, stages)
    either(take, out, lambda: got[...], lambda: had[...])


def forward(n, m, stage, stages, piv, *refs):
    f = facts(n, m, 2, piv)
    count = len(refs) // 3
    had, got, out = (pair(refs[i * count : (i + 1) * count]) for i in range(3))
    for q in range(2):
        take = bit_of(f, f["c"][q], stage, stages)
        either(take, out[q], lambda: got[q][...], lambda: had[q][...])


def hand_on(n, m, stride, had, got, extra):
    r = lax.axis_index("prow").astype(jnp.int32)
    low = (r & (2 * stride - 1)) == stride
    high = ((n - 1 - r) & (2 * stride - 1)) == stride
    either(jnp.logical_or(low, high), extra, lambda: got[...], lambda: had[...])


def dot(left, right):
    return jnp.dot(left, right, preferred_element_type=jnp.float32)


def settle_extra(n, m, piv, inv, *refs):
    had, out = refs[:-1], refs[-1]
    f = facts(n, m, 2, piv)
    r = f["r"]
    stages = len(had) - 1
    for which in range(2):
        place = r if which == 0 else n - 1 - r
        low_is_v = f["low_first"] if which == 0 else jnp.logical_not(f["low_first"])
        for s in range(stages + 1):
            if s == 0:
                here = place == 0
            else:
                here = (place & (2 * (n >> s) - 1)) == (n >> s)

            @pl.when(jnp.logical_and(here, low_is_v))
            def _():
                out[0] = had[s][...]

            @pl.when(jnp.logical_and(here, jnp.logical_not(low_is_v)))
            def _():
                out[1] = had[s][...]

    out[1] = dot(out[1], inv[0]).astype(out.dtype)


def multiply(n, m, stages, piv, inv, vl, sib_vl, *refs):
    panels, out, v = refs[:-2], refs[-2], refs[-1]
    f = facts(n, m, 2, piv)
    half = vl.shape[1]
    v[rows(f["core"], half), :] = vl[0]
    v[rows(1 - f["core"], half), :] = sib_vl[0]
    count = len(panels) // 2
    for q in range(2):
        take = bit_of(f, f["c"][q], stages - 1, stages)
        had, got = pair(panels[:count])[q], pair(panels[count:])[q]
        either(take, out.at[q], lambda: got[...], lambda: had[...])
    for k in range(out.shape[1]):
        m0 = dot(out[0, k], inv[0]).astype(out.dtype)
        p1 = (out[1, k].astype(jnp.float32) - dot(m0, v[...])).astype(out.dtype)
        out[0, k] = m0
        out[1, k] = dot(p1, inv[1]).astype(out.dtype)


def settle_rows(n, m, piv, vl, sib_vl, leaving, moved, *refs):
    hops, upper, lefts = refs[:-2], refs[-2], refs[-1]
    width = leaving.shape[0]
    half = width // 2
    f = facts(n, m, 2, piv)
    r = f["r"]
    for which in range(2):
        place = r if which == 0 else n - 1 - r
        slot = jnp.where(f["low_first"], which, 1 - which)
        for h in range(n):

            @pl.when(place == h)
            def _():
                if h == 0:
                    upper[slot] = leaving[...]
                elif h == 1:
                    upper[slot] = moved[...]
                else:
                    upper[slot, :half, :] = hops[2 * (h - 2)][...]
                    upper[slot, half:, :] = hops[2 * (h - 2) + 1][...]

    lefts[rows(f["core"], half), :] = vl[1]
    lefts[rows(1 - f["core"], half), :] = sib_vl[1]
    for p in range(2):
        cut = slice(p * half, (p + 1) * half)
        fresh = upper[1, cut, :].astype(jnp.float32) - dot(lefts[cut, :], upper[0])
        upper[1, cut, :] = fresh.astype(upper.dtype)


def update(f, upper, mine, sib, at, old, new):
    half = old.shape[0] // 2
    for p in range(2):
        part = jnp.where(f["core"] == p, 0, 1)
        cut = slice(p * half, (p + 1) * half)

        def left(q):
            return jnp.where(part == 0, mine[(q, *at)], sib[(q, *at)])

        m0, m1 = left(0), left(1)

        @pl.when(f["j"] == f["c"][0])
        def _():
            new[cut, :] = m0

        @pl.when(f["j"] == f["c"][1])
        def _():
            new[cut, :] = m1

        @pl.when(jnp.logical_and(f["j"] != f["c"][0], f["j"] != f["c"][1]))
        def _():
            w = (old[cut, :].astype(jnp.float32) - dot(m0, upper[0])).astype(new.dtype)
            w = w.astype(jnp.float32) - dot(m1, upper[1])
            new[cut, :] = w.astype(new.dtype)


def update_stays(n, m, piv, upper, mine, sib, raw, out, new, sems):
    rb = raw.shape[0]
    f = facts(n, m, rb, piv)
    copies = []
    for k in range(rb - 1):
        update(f, upper, mine, sib, (k,), raw.at[k], new.at[k])
        copies.append(pltpu.make_async_copy(new.at[k], out.at[f["slots"][k]], sems.at[k]))
        copies[-1].start()
    for copy in copies:
        copy.wait()


def update_third(n, m, piv, upper, lefts, mine, sib, raw, moved, so_far, out, old, new, sem):
    del so_far
    rb = raw.shape[0]
    f = facts(n, m, rb, piv)
    low_first = f["low_first"]
    first = jnp.where(low_first, f["is_low"], f["is_high"])
    second = jnp.where(low_first, f["is_high"], f["is_low"])

    @pl.when(first)
    def _():
        new[...] = upper[0]

    @pl.when(second)
    def _():
        either(f["j"] == f["c"][0], new, lambda: lefts[...], lambda: upper[1])

    @pl.when(jnp.logical_not(jnp.logical_or(first, second)))
    def _():
        either(f["is_end"], old, lambda: moved[...], lambda: raw[rb - 1])
        update(f, upper, mine, sib, (0,), old, new)

    copy = pltpu.make_async_copy(new, out.at[f["slots"][rb - 1]], sem)
    copy.start()
    copy.wait()


def local(matrix, pattern, inverses, pivots):
    n = lax.axis_size("prow")
    m = lax.axis_size("pcol")
    rb, width = matrix.shape[0], matrix.shape[1]
    half = width // 2
    chips = m // 2
    stages = chips.bit_length() - 1
    dt = matrix.dtype
    blocks = matrix.reshape(rb, width, width)

    def call(kernel, shapes, specs, *operands, scratch=(), aliases=(), products=0, place=VMEM, after=(), name=None, weight=0):
        outs = [jax.ShapeDtypeStruct(s, dt) for s in shapes]
        count = len(operands)
        scratch = [pltpu.VMEM(s, dt) if isinstance(s, tuple) else s for s in scratch]

        def body(*refs):
            kernel(n, m, *refs[:count], *refs[count + len(after) :])

        kinds = {"s": SMEM, "v": VMEM, "a": ANY}
        specs = [kinds[k] for k in specs.ljust(count, "v")] + [ANY] * len(after)
        result = pl.pallas_call(
            body,
            out_shape=outs,
            in_specs=specs,
            out_specs=[place] * len(outs),
            scratch_shapes=scratch,
            input_output_aliases=dict(aliases),
            compiler_params=GRANT,
            name=name or kernel.__name__,
            cost_estimate=pl.CostEstimate(
                flops=int(products * 2 * width**3),
                bytes_accessed=weight + sum(a.size * a.dtype.itemsize for a in operands),
                transcendentals=0,
            ),
        )(*operands, *after)
        return result if len(result) > 1 else result[0]

    def along(name, pairs, value):
        with jax.named_scope(name):
            return lax.ppermute(value, "prow", pairs)

    def sibling(name, value):
        with jax.named_scope(name):
            return lax.ppermute(value, "pcol", [(i, i ^ 1) for i in range(m)])

    def across(name, stage, value):
        pairs = []
        for i in range(m):
            bit = stage if i % 2 == 0 else stages - 1 - stage
            pairs.append((i, i ^ (2 << bit)))
        with jax.named_scope(name):
            return lax.ppermute(value, "pcol", pairs)

    def cross(name, s, values):
        return [across(name + str(s) + "ab"[i], s, v) for i, v in enumerate(values)]

    def passing(name, kernel, values, got, after=()):
        for s in range(stages - 1):
            step = lambda _n, _m, *refs: kernel(n, m, s, stages, *refs)
            shapes = [v.shape for v in values]
            values = call(
                step, shapes, "s", pivots, *values, *got, after=after, name="pass_" + name
            )
            values = [values] if len(shapes) == 1 else list(values)
            got = cross(name, s + 1, values)
        return [*values, *got]

    square, strip = (width, width), (half, width)
    raw, leaving, other = call(
        prepare,
        [(rb, *square), square, (rb, *strip)],
        "ss",
        pivots,
        pattern.T,
        blocks,
    )
    moved = along("swap", [(0, 1), (n - 1, n - 2), (n // 2, 0), (n // 2 - 1, n - 1)], leaving)
    early = sibling("sib_early", other)

    extra = call(pick_extra, [strip], "s", pivots, raw, early)
    panel = call(pick, [(rb - 1, *strip)] * 2, "s", pivots, raw, early, after=[extra])
    got_extra = cross("extra", 0, [extra])
    got_stays = cross("stays", 0, panel)
    had, got = passing("extra", forward_extra, [extra], got_extra, after=[panel[0]])
    step = lambda _n, _m, *refs: forward_extra(n, m, stages - 1, stages, *refs)
    extra_here = call(
        step, [strip], "s", pivots, had, got, after=[got_stays[0]], name="extra_here"
    )
    moved, *parts = call(relay, [square, strip, strip], "", moved, after=[extra_here])

    sib_moved = sibling("sib_moved", moved)
    third = call(
        pick_third, [(2, 1, *strip)], "s", pivots, raw, early, moved, sib_moved
    )
    got_third = cross("third", 0, [third])
    stays = passing("stays", forward, panel, got_stays, after=[third])

    hops = []
    for h in range(1, n - 1):
        pairs = [(h, h + 1), (n - 1 - h, n - 2 - h)]
        parts = [along("row" + str(h) + "ab"[i], pairs, part) for i, part in enumerate(parts)]
        hops += parts

    came = [extra_here]
    send = extra_here
    stride = n // 2
    while stride:
        pairs = []
        for i in range(0, n, 2 * stride):
            pairs += [(i, i + stride), (n - 1 - i, n - 1 - i - stride)]
        got = along("extra_z" + str(stride), pairs, send)
        came.append(got)
        if stride > 1:
            step = lambda _n, _m, *refs: hand_on(n, m, stride, *refs)
            send = call(
                step,
                [strip],
                "",
                send,
                got,
                name="hand_on",
                after=[stays[0]],
            )
        stride //= 2
    third = passing("third", forward, [third], got_third, after=[send, hops[0]])
    vl = call(
        settle_extra,
        [(2, *strip)],
        "s",
        pivots,
        inverses,
        *came,
        products=0.5,
        after=[third[0], hops[1]],
    )
    sib_vl = sibling("sib_vl", vl)

    step = lambda _n, _m, *refs: multiply(n, m, stages, *refs)
    mine = call(
        step,
        [(2, rb - 1, *strip)],
        "s",
        pivots,
        inverses,
        vl,
        sib_vl,
        *stays,
        scratch=[square],
        products=3 * (rb - 1) / 2,
        name="multiply_stays",
        after=[hops[2], third[1]],
    )
    sib_mine = sibling("sib_mine", mine)
    upper, lefts = call(
        settle_rows,
        [(2, *square), square],
        "s",
        pivots,
        vl,
        sib_vl,
        leaving,
        moved,
        *hops,
        products=1,
        after=[mine],
    )
    mine_third = call(
        step,
        [(2, 1, *strip)],
        "s",
        pivots,
        inverses,
        vl,
        sib_vl,
        *third,
        scratch=[square],
        products=1.5,
        after=[upper],
        name="multiply_third",
    )
    sib_third = sibling("sib_third", mine_third)
    result = call(
        update_stays,
        [blocks.shape],
        "s",
        pivots,
        upper,
        mine,
        sib_mine,
        raw,
        scratch=[(rb - 1, *square), pltpu.SemaphoreType.DMA((rb - 1,))],
        products=2 * (rb - 1),
        place=ANY,
    )
    result = call(
        update_third,
        [blocks.shape],
        "svvvvvva",
        pivots,
        upper,
        lefts,
        mine_third,
        sib_third,
        raw,
        moved,
        result,
        scratch=[square, square, pltpu.SemaphoreType.DMA],
        aliases={7: 0},
        products=2,
        place=ANY,
    )
    return result.reshape(matrix.shape)


def solution(mesh):
    placed = (P(None, "prow", None, "pcol"), P(), P(), P())
    return jax.shard_map(
        local, mesh=mesh, in_specs=placed, out_specs=P(None, "prow", None, "pcol"), check_vma=False
    )
```

```python
import functools

import jax
import jax.numpy as jnp
from jax import lax
from jax.experimental import pallas as pl
from jax.experimental.pallas import tpu as pltpu
from jax.sharding import PartitionSpec as P

SMEM = pl.BlockSpec(memory_space=pltpu.SMEM)
VMEM = pl.BlockSpec(memory_space=pltpu.VMEM)
ANY = pl.BlockSpec(memory_space=pl.ANY)
GRANT = pltpu.CompilerParams(vmem_limit_bytes=24 * 2**20)


def facts(n, m, rb, pivots):
    f = {}
    r = f["r"] = lax.axis_index("prow").astype(jnp.int32)
    j = f["j"] = lax.axis_index("pcol").astype(jnp.int32)
    f["core"] = j & 1
    f["chip"] = j >> 1
    low_first = f["low_first"] = pivots[0, 1] == 0
    shift = n.bit_length() - 1
    a_low = jnp.where(low_first, pivots[0, 0], pivots[1, 0]) >> shift
    a_high = jnp.where(low_first, pivots[1, 0], pivots[0, 0]) >> shift
    f["c"] = [pivots[0, 2], pivots[1, 2]]
    is_low, is_high = r == n // 2, r == n // 2 - 1
    f["is_low"], f["is_high"] = is_low, is_high
    f["is_end"] = jnp.logical_or(r == 0, r == n - 1)
    out = jnp.where(is_low, a_low, jnp.where(is_high, a_high, jnp.where(r == 0, 0, rb - 1)))
    f["slots"] = []
    for k in range(rb):
        slot = out + (1 + k)
        f["slots"].append(jnp.where(slot >= rb, slot - rb, slot))
    f["cx"] = jnp.where((r == 0) == low_first, pivots[1, 2], pivots[0, 2])
    return f


def either(cond, out_ref, yes, no):
    @pl.when(cond)
    def _():
        out_ref[...] = yes()

    @pl.when(jnp.logical_not(cond))
    def _():
        out_ref[...] = no()


def rows(part, half):
    return pl.ds(pl.multiple_of(part * half, half), half)


def prepare(n, m, piv, pat, mat, raw, leave_top, leave_low, other):
    rb, width = mat.shape[0], mat.shape[1]
    f = facts(n, m, rb, piv)
    cut = rows(1 - f["core"], width // 2)
    for k in reversed(range(rb)):
        slot = f["slots"][k]
        keep = pat[f["j"], slot * n + f["r"]] != 0
        zero = lambda: jnp.zeros((width, width), mat.dtype)
        either(keep, raw.at[k], lambda: mat[slot], zero)
        if k == rb - 1:
            leave_top[...] = raw[k, : width // 2, :]
            leave_low[...] = raw[k, width // 2 :, :]
        other[k] = raw[k, cut, :]


def pick_extra(n, m, piv, raw, sib, extra):
    rb, width = raw.shape[0], raw.shape[1]
    f = facts(n, m, rb, piv)
    cut = rows(f["core"], width // 2)
    hit = (f["cx"] & 1) == f["core"]
    either(hit, extra, lambda: raw[rb - 1, cut, :], lambda: sib[rb - 1])


def pair(refs):
    return [refs[0].at[q] for q in range(2)] if len(refs) == 1 else list(refs)


def pick(n, m, piv, raw, sib, *panel):
    rb, width = raw.shape[0], raw.shape[1]
    f = facts(n, m, rb, piv)
    cut = rows(f["core"], width // 2)
    for q in range(2):
        hit = (f["c"][q] & 1) == f["core"]
        for k in range(rb - 1):
            either(hit, pair(panel)[q].at[k], lambda: raw[k, cut, :], lambda: sib[k])


def pick_third(n, m, piv, raw, sib, top, low, sib_moved, panel):
    rb, width = raw.shape[0], raw.shape[1]
    f = facts(n, m, rb, piv)
    cut = rows(f["core"], width // 2)
    for q in range(2):
        hit = (f["c"][q] & 1) == f["core"]
        new = jnp.logical_and(f["is_end"], hit)

        @pl.when(jnp.logical_and(new, f["core"] == 0))
        def _():
            panel[q, 0] = top[...]

        @pl.when(jnp.logical_and(new, f["core"] == 1))
        def _():
            panel[q, 0] = low[...]

        @pl.when(jnp.logical_and(f["is_end"], jnp.logical_not(hit)))
        def _():
            panel[q, 0] = sib_moved[...]

        @pl.when(jnp.logical_not(f["is_end"]))
        def _():
            either(hit, panel.at[q, 0], lambda: raw[rb - 1, cut, :], lambda: sib[rb - 1])


def relay(n, m, stride, leave_low, top, low, other, send):
    core = lax.axis_index("pcol").astype(jnp.int32) & 1
    either(core == 0, other, lambda: low[...], lambda: top[...])
    hand_on(n, m, stride, leave_low, low, send)


def bit_of(f, column, stage, stages):
    apart = f["chip"] ^ (column >> 1)
    bit = jnp.where(f["core"] == 0, stage, stages - 1 - stage)
    return ((apart >> bit) & 1) == 1


def forward_extra(n, m, stage, stages, piv, had, got, out):
    f = facts(n, m, 2, piv)
    take = bit_of(f, f["cx"], stage, stages)
    either(take, out, lambda: got[...], lambda: had[...])


def forward(n, m, stage, stages, piv, *refs):
    f = facts(n, m, 2, piv)
    count = len(refs) // 3
    had, got, out = (pair(refs[i * count : (i + 1) * count]) for i in range(3))
    for q in range(2):
        take = bit_of(f, f["c"][q], stage, stages)
        either(take, out[q], lambda: got[q][...], lambda: had[q][...])


def hand_on(n, m, stride, had, got, extra):
    r = lax.axis_index("prow").astype(jnp.int32)
    low = (r & (2 * stride - 1)) == stride
    high = ((n - 1 - r) & (2 * stride - 1)) == stride
    either(jnp.logical_or(low, high), extra, lambda: got[...], lambda: had[...])


def dot(left, right):
    return jnp.dot(left, right, preferred_element_type=jnp.float32)


def settle_extra(n, m, piv, inv, *refs):
    had, out = refs[:-1], refs[-1]
    f = facts(n, m, 2, piv)
    r = f["r"]
    stages = len(had) - 1
    for which in range(2):
        place = r if which == 0 else n - 1 - r
        low_is_v = f["low_first"] if which == 0 else jnp.logical_not(f["low_first"])
        for s in range(stages + 1):
            if s == 0:
                here = place == 0
            else:
                here = (place & (2 * (n >> s) - 1)) == (n >> s)

            @pl.when(jnp.logical_and(here, low_is_v))
            def _():
                out[0] = had[s][...]

            @pl.when(jnp.logical_and(here, jnp.logical_not(low_is_v)))
            def _():
                out[1] = had[s][...]

    out[1] = dot(out[1], inv[0]).astype(out.dtype)


def multiply(n, m, stages, piv, inv, vl, sib_vl, *refs):
    panels, out, v = refs[:-2], refs[-2], refs[-1]
    f = facts(n, m, 2, piv)
    half = vl.shape[1]
    v[rows(f["core"], half), :] = vl[0]
    v[rows(1 - f["core"], half), :] = sib_vl[0]
    count = len(panels) // 2
    for q in range(2):
        take = bit_of(f, f["c"][q], stages - 1, stages)
        had, got = pair(panels[:count])[q], pair(panels[count:])[q]
        either(take, out.at[q], lambda: got[...], lambda: had[...])
    for k in range(out.shape[1]):
        m0 = dot(out[0, k], inv[0]).astype(out.dtype)
        p1 = (out[1, k].astype(jnp.float32) - dot(m0, v[...])).astype(out.dtype)
        out[0, k] = m0
        out[1, k] = dot(p1, inv[1]).astype(out.dtype)


def settle_rows(n, m, piv, vl, sib_vl, *refs):
    tops, upper, lefts = refs[:-2], refs[-2], refs[-1]
    count = len(tops) // 2
    half, width = tops[0].shape
    f = facts(n, m, 2, piv)
    r = f["r"]
    for which in range(2):
        place = r if which == 0 else n - 1 - r
        slot = jnp.where(f["low_first"], which, 1 - which)
        for s in range(count):
            here = place == 0 if s == 0 else (place & (2 * (n >> s) - 1)) == (n >> s)

            @pl.when(here)
            def _():
                upper[slot, :half, :] = tops[s][...]
                upper[slot, half:, :] = tops[count + s][...]

    lefts[rows(f["core"], half), :] = vl[1]
    lefts[rows(1 - f["core"], half), :] = sib_vl[1]
    for p in range(2):
        cut = slice(p * half, (p + 1) * half)
        fresh = upper[1, cut, :].astype(jnp.float32) - dot(lefts[cut, :], upper[0])
        upper[1, cut, :] = fresh.astype(upper.dtype)


def update(f, upper, mine, sib, at, old, new):
    half = old.shape[0] // 2
    for p in range(2):
        part = jnp.where(f["core"] == p, 0, 1)
        cut = slice(p * half, (p + 1) * half)

        def left(q):
            return jnp.where(part == 0, mine[(q, *at)], sib[(q, *at)])

        m0, m1 = left(0), left(1)

        @pl.when(f["j"] == f["c"][0])
        def _():
            new[cut, :] = m0

        @pl.when(f["j"] == f["c"][1])
        def _():
            new[cut, :] = m1

        @pl.when(jnp.logical_and(f["j"] != f["c"][0], f["j"] != f["c"][1]))
        def _():
            w = (old[cut, :].astype(jnp.float32) - dot(m0, upper[0])).astype(new.dtype)
            w = w.astype(jnp.float32) - dot(m1, upper[1])
            new[cut, :] = w.astype(new.dtype)


def update_stays(n, m, piv, upper, mine, sib, raw, out, new, sems):
    rb = raw.shape[0]
    f = facts(n, m, rb, piv)
    copies = []
    for k in range(rb - 1):
        update(f, upper, mine, sib, (k,), raw.at[k], new.at[k])
        copies.append(pltpu.make_async_copy(new.at[k], out.at[f["slots"][k]], sems.at[k]))
        copies[-1].start()
    for copy in copies:
        copy.wait()


def update_third(n, m, piv, upper, lefts, mine, sib, raw, top, low, so_far, out, old, new, sem):
    del so_far
    rb = raw.shape[0]
    f = facts(n, m, rb, piv)
    low_first = f["low_first"]
    first = jnp.where(low_first, f["is_low"], f["is_high"])
    second = jnp.where(low_first, f["is_high"], f["is_low"])

    @pl.when(first)
    def _():
        new[...] = upper[0]

    @pl.when(second)
    def _():
        either(f["j"] == f["c"][0], new, lambda: lefts[...], lambda: upper[1])

    @pl.when(jnp.logical_not(jnp.logical_or(first, second)))
    def _():
        half = top.shape[0]
        either(f["is_end"], old.at[:half], lambda: top[...], lambda: raw[rb - 1, :half, :])
        either(f["is_end"], old.at[half:], lambda: low[...], lambda: raw[rb - 1, half:, :])
        update(f, upper, mine, sib, (0,), old, new)

    copy = pltpu.make_async_copy(new, out.at[f["slots"][rb - 1]], sem)
    copy.start()
    copy.wait()


def local(matrix, pattern, inverses, pivots):
    n = lax.axis_size("prow")
    m = lax.axis_size("pcol")
    rb, width = matrix.shape[0], matrix.shape[1]
    half = width // 2
    chips = m // 2
    stages = chips.bit_length() - 1
    dt = matrix.dtype
    blocks = matrix.reshape(rb, width, width)

    def call(kernel, shapes, specs, *operands, scratch=(), aliases=(), products=0, place=VMEM, after=(), name=None, weight=0):
        outs = [jax.ShapeDtypeStruct(s, dt) for s in shapes]
        count = len(operands)
        scratch = [pltpu.VMEM(s, dt) if isinstance(s, tuple) else s for s in scratch]

        def body(*refs):
            kernel(n, m, *refs[:count], *refs[count + len(after) :])

        kinds = {"s": SMEM, "v": VMEM, "a": ANY}
        specs = [kinds[k] for k in specs.ljust(count, "v")] + [ANY] * len(after)
        result = pl.pallas_call(
            body,
            out_shape=outs,
            in_specs=specs,
            out_specs=[place] * len(outs),
            scratch_shapes=scratch,
            input_output_aliases=dict(aliases),
            compiler_params=GRANT,
            name=name or kernel.__name__,
            cost_estimate=pl.CostEstimate(
                flops=int(products * 2 * width**3),
                bytes_accessed=weight + sum(a.size * a.dtype.itemsize for a in operands),
                transcendentals=0,
            ),
        )(*operands, *after)
        return result if len(result) > 1 else result[0]

    def along(name, pairs, value):
        with jax.named_scope(name):
            return lax.ppermute(value, "prow", pairs)

    def sibling(name, value):
        with jax.named_scope(name):
            return lax.ppermute(value, "pcol", [(i, i ^ 1) for i in range(m)])

    def across(name, stage, value):
        pairs = []
        for i in range(m):
            bit = stage if i % 2 == 0 else stages - 1 - stage
            pairs.append((i, i ^ (2 << bit)))
        with jax.named_scope(name):
            return lax.ppermute(value, "pcol", pairs)

    def cross(name, s, values):
        return [across(name + str(s) + "ab"[i], s, v) for i, v in enumerate(values)]

    def passing(name, kernel, values, got, after=()):
        for s in range(stages - 1):
            step = lambda _n, _m, *refs: kernel(n, m, s, stages, *refs)
            shapes = [v.shape for v in values]
            values = call(
                step, shapes, "s", pivots, *values, *got, after=after, name="pass_" + name
            )
            values = [values] if len(shapes) == 1 else list(values)
            got = cross(name, s + 1, values)
        return [*values, *got]

    square, strip = (width, width), (half, width)
    raw, *leaving, other = call(
        prepare,
        [(rb, *square), strip, strip, (rb, *strip)],
        "ss",
        pivots,
        pattern.T,
        blocks,
    )
    early = sibling("sib_early", other)
    exchange = [(0, n // 2), (n - 1, n // 2 - 1), (n // 2, 0), (n // 2 - 1, n - 1)]
    moved = [along("swap" + "ab"[i], exchange, leaving[i]) for i in range(2)]

    def split(stride):
        pairs = []
        for i in range(0, n, 2 * stride):
            pairs += [(i, i + stride), (n - 1 - i, n - 1 - i - stride)]
        return pairs

    extra = call(pick_extra, [strip], "s", pivots, raw, early)
    panel = call(pick, [(rb - 1, *strip)] * 2, "s", pivots, raw, early, after=[extra])
    got_extra = cross("extra", 0, [extra])
    got_stays = cross("stays", 0, panel)
    had, got = passing("extra", forward_extra, [extra], got_extra, after=[panel[0]])
    hand = lambda stride: lambda _n, _m, *refs: hand_on(n, m, stride, *refs)
    sends = [
        call(hand(n // 2), [strip], "", leaving[0], moved[0], name="hand_on_a", after=[had])
    ]
    step = lambda _n, _m, *refs: forward_extra(n, m, stages - 1, stages, *refs)
    extra_here = call(step, [strip], "s", pivots, had, got, after=[sends[0]], name="extra_here")
    stays = passing("stays", forward, panel, got_stays, after=[extra_here])
    step = lambda _n, _m, *refs: relay(n, m, n // 2, *refs)
    other_moved, send = call(
        step, [strip] * 2, "", leaving[1], *moved, name="relay", after=[stays[0]]
    )
    sends.append(send)
    after_relay = send

    arrived = [[leaving[i], moved[i]] for i in range(2)]
    stride = n // 4
    while stride:
        for i in range(2):
            got = along("row" + str(stride) + "ab"[i], split(stride), sends[i])
            arrived[i].append(got)
            if stride > 1:
                sends[i] = call(hand(stride), [strip], "", sends[i], got, name="hand_on_row")
        stride //= 2

    came = [extra_here]
    send = extra_here
    stride = n // 2
    while stride:
        got = along("extra_z" + str(stride), split(stride), send)
        came.append(got)
        if stride > 1:
            send = call(hand(stride), [strip], "", send, got, name="hand_on", after=[after_relay])
        stride //= 2
    sib_moved = sibling("sib_moved", other_moved)
    third = call(
        pick_third, [(2, 1, *strip)], "s", pivots, raw, early, *moved, sib_moved, after=[send, stays[2]]
    )
    got_third = cross("third", 0, [third])

    third = passing("third", forward, [third], got_third, after=[arrived[0][2], *stays[2:]])
    vl = call(
        settle_extra,
        [(2, *strip)],
        "s",
        pivots,
        inverses,
        *came,
        products=0.5,
        after=[third[0]],
    )
    sib_vl = sibling("sib_vl", vl)

    upper, lefts = call(
        settle_rows,
        [(2, *square), square],
        "s",
        pivots,
        vl,
        sib_vl,
        *arrived[0],
        *arrived[1],
        products=1,
    )
    step = lambda _n, _m, *refs: multiply(n, m, stages, *refs)
    mine = call(
        step,
        [(2, rb - 1, *strip)],
        "s",
        pivots,
        inverses,
        vl,
        sib_vl,
        *stays,
        scratch=[square],
        products=3 * (rb - 1) / 2,
        name="multiply_stays",
        after=[upper],
    )
    sib_mine = sibling("sib_mine", mine)
    mine_third = call(
        step,
        [(2, 1, *strip)],
        "s",
        pivots,
        inverses,
        vl,
        sib_vl,
        *third,
        scratch=[square],
        products=1.5,
        after=[mine],
        name="multiply_third",
    )
    sib_third = sibling("sib_third", mine_third)
    result = call(
        update_stays,
        [blocks.shape],
        "s",
        pivots,
        upper,
        mine,
        sib_mine,
        raw,
        scratch=[(rb - 1, *square), pltpu.SemaphoreType.DMA((rb - 1,))],
        products=2 * (rb - 1),
        place=ANY,
    )
    result = call(
        update_third,
        [blocks.shape],
        "svvvvvvva",
        pivots,
        upper,
        lefts,
        mine_third,
        sib_third,
        raw,
        *moved,
        result,
        scratch=[square, square, pltpu.SemaphoreType.DMA],
        aliases={8: 0},
        products=2,
        place=ANY,
    )
    return result.reshape(matrix.shape)


def solution(mesh):
    placed = (P(None, "prow", None, "pcol"), P(), P(), P())
    return jax.shard_map(
        local, mesh=mesh, in_specs=placed, out_specs=P(None, "prow", None, "pcol"), check_vma=False
    )
```

```python
import functools

import jax
import jax.numpy as jnp
from jax import lax
from jax.experimental import pallas as pl
from jax.experimental.pallas import tpu as pltpu
from jax.sharding import PartitionSpec as P

SMEM = pl.BlockSpec(memory_space=pltpu.SMEM)
VMEM = pl.BlockSpec(memory_space=pltpu.VMEM)
ANY = pl.BlockSpec(memory_space=pl.ANY)
GRANT = pltpu.CompilerParams(vmem_limit_bytes=24 * 2**20)


def facts(n, m, rb, pivots):
    f = {}
    r = f["r"] = lax.axis_index("prow").astype(jnp.int32)
    j = f["j"] = lax.axis_index("pcol").astype(jnp.int32)
    f["core"] = j & 1
    f["chip"] = j >> 1
    low_first = f["low_first"] = pivots[0, 1] == 0
    shift = n.bit_length() - 1
    a_low = jnp.where(low_first, pivots[0, 0], pivots[1, 0]) >> shift
    a_high = jnp.where(low_first, pivots[1, 0], pivots[0, 0]) >> shift
    f["c"] = [pivots[0, 2], pivots[1, 2]]
    is_low, is_high = r == n // 2, r == n // 2 - 1
    f["is_low"], f["is_high"] = is_low, is_high
    f["is_end"] = jnp.logical_or(r == 0, r == n - 1)
    out = jnp.where(is_low, a_low, jnp.where(is_high, a_high, jnp.where(r == 0, 0, rb - 1)))
    f["slots"] = []
    for k in range(rb):
        slot = out + (1 + k)
        f["slots"].append(jnp.where(slot >= rb, slot - rb, slot))
    f["cx"] = jnp.where((r == 0) == low_first, pivots[1, 2], pivots[0, 2])
    return f


def either(cond, out_ref, yes, no):
    @pl.when(cond)
    def _():
        out_ref[...] = yes()

    @pl.when(jnp.logical_not(cond))
    def _():
        out_ref[...] = no()


def rows(part, half):
    return pl.ds(pl.multiple_of(part * half, half), half)


def prepare(n, m, piv, pat, mat, raw, leaving, other):
    rb, width = mat.shape[0], mat.shape[1]
    f = facts(n, m, rb, piv)
    cut = rows(1 - f["core"], width // 2)
    for k in reversed(range(rb)):
        slot = f["slots"][k]
        keep = pat[f["j"], slot * n + f["r"]] != 0
        zero = lambda: jnp.zeros((width, width), mat.dtype)
        either(keep, raw.at[k], lambda: mat[slot], zero)
        if k == rb - 1:
            leaving[...] = raw[k]
        other[k] = raw[k, cut, :]


def pick_extra(n, m, piv, raw, sib, extra):
    rb, width = raw.shape[0], raw.shape[1]
    f = facts(n, m, rb, piv)
    cut = rows(f["core"], width // 2)
    hit = (f["cx"] & 1) == f["core"]
    either(hit, extra, lambda: raw[rb - 1, cut, :], lambda: sib[rb - 1])


def pair(refs):
    return [refs[0].at[q] for q in range(2)] if len(refs) == 1 else list(refs)


def pick(n, m, piv, raw, sib, *panel):
    rb, width = raw.shape[0], raw.shape[1]
    f = facts(n, m, rb, piv)
    cut = rows(f["core"], width // 2)
    for q in range(2):
        hit = (f["c"][q] & 1) == f["core"]
        for k in range(rb - 1):
            either(hit, pair(panel)[q].at[k], lambda: raw[k, cut, :], lambda: sib[k])


def pick_third(n, m, piv, raw, sib, moved, sib_moved, panel):
    rb, width = raw.shape[0], raw.shape[1]
    f = facts(n, m, rb, piv)
    cut = rows(f["core"], width // 2)
    for q in range(2):
        hit = (f["c"][q] & 1) == f["core"]

        @pl.when(f["is_end"])
        def _():
            either(hit, panel.at[q, 0], lambda: moved[cut, :], lambda: sib_moved[...])

        @pl.when(jnp.logical_not(f["is_end"]))
        def _():
            either(hit, panel.at[q, 0], lambda: raw[rb - 1, cut, :], lambda: sib[rb - 1])


def relay(n, m, stride, leaving, moved, other, send):
    core = lax.axis_index("pcol").astype(jnp.int32) & 1
    other[...] = moved[rows(1 - core, moved.shape[0] // 2), :]
    hand_on(n, m, stride, leaving, moved, send)


def bit_of(f, column, stage, stages):
    apart = f["chip"] ^ (column >> 1)
    bit = jnp.where(f["core"] == 0, stage, stages - 1 - stage)
    return ((apart >> bit) & 1) == 1


def forward_extra(n, m, stage, stages, piv, had, got, out):
    f = facts(n, m, 2, piv)
    take = bit_of(f, f["cx"], stage, stages)
    either(take, out, lambda: got[...], lambda: had[...])


def forward(n, m, stage, stages, piv, *refs):
    f = facts(n, m, 2, piv)
    count = len(refs) // 3
    had, got, out = (pair(refs[i * count : (i + 1) * count]) for i in range(3))
    for q in range(2):
        take = bit_of(f, f["c"][q], stage, stages)
        either(take, out[q], lambda: got[q][...], lambda: had[q][...])


def hand_on(n, m, stride, had, got, extra):
    r = lax.axis_index("prow").astype(jnp.int32)
    low = (r & (2 * stride - 1)) == stride
    high = ((n - 1 - r) & (2 * stride - 1)) == stride
    either(jnp.logical_or(low, high), extra, lambda: got[...], lambda: had[...])


def dot(left, right):
    return jnp.dot(left, right, preferred_element_type=jnp.float32)


def settle_extra(n, m, piv, inv, *refs):
    had, out = refs[:-1], refs[-1]
    f = facts(n, m, 2, piv)
    r = f["r"]
    stages = len(had) - 1
    for which in range(2):
        place = r if which == 0 else n - 1 - r
        low_is_v = f["low_first"] if which == 0 else jnp.logical_not(f["low_first"])
        for s in range(stages + 1):
            if s == 0:
                here = place == 0
            else:
                here = (place & (2 * (n >> s) - 1)) == (n >> s)

            @pl.when(jnp.logical_and(here, low_is_v))
            def _():
                out[0] = had[s][...]

            @pl.when(jnp.logical_and(here, jnp.logical_not(low_is_v)))
            def _():
                out[1] = had[s][...]

    out[1] = dot(out[1], inv[0]).astype(out.dtype)


def multiply(n, m, stages, piv, inv, vl, sib_vl, *refs):
    panels, third, third_got, out, v = refs[:-4], refs[-4], refs[-3], refs[-2], refs[-1]
    f = facts(n, m, 2, piv)
    half = vl.shape[1]
    v[rows(f["core"], half), :] = vl[0]
    v[rows(1 - f["core"], half), :] = sib_vl[0]
    count = out.shape[1] - 1
    for q in range(2):
        take = bit_of(f, f["c"][q], stages - 1, stages)
        had, got = panels[q], panels[2 + q]
        either(take, out.at[q, :count], lambda: got[...], lambda: had[...])
        either(take, out.at[q, count], lambda: third_got[q, 0], lambda: third[q, 0])
    for k in range(count + 1):
        m0 = dot(out[0, k], inv[0]).astype(out.dtype)
        p1 = (out[1, k].astype(jnp.float32) - dot(m0, v[...])).astype(out.dtype)
        out[0, k] = m0
        out[1, k] = dot(p1, inv[1]).astype(out.dtype)


def settle_rows(n, m, piv, vl, sib_vl, *refs):
    came, upper, lefts = refs[:-2], refs[-2], refs[-1]
    half = came[0].shape[0] // 2
    f = facts(n, m, 2, piv)
    r = f["r"]
    for which in range(2):
        place = r if which == 0 else n - 1 - r
        slot = jnp.where(f["low_first"], which, 1 - which)
        for s in range(len(came)):
            here = place == 0 if s == 0 else (place & (2 * (n >> s) - 1)) == (n >> s)

            @pl.when(here)
            def _():
                upper[slot] = came[s][...]

    lefts[rows(f["core"], half), :] = vl[1]
    lefts[rows(1 - f["core"], half), :] = sib_vl[1]
    for p in range(2):
        cut = slice(p * half, (p + 1) * half)
        fresh = upper[1, cut, :].astype(jnp.float32) - dot(lefts[cut, :], upper[0])
        upper[1, cut, :] = fresh.astype(upper.dtype)


def update(f, upper, mine, sib, at, old, new):
    half = old.shape[0] // 2
    for p in range(2):
        part = jnp.where(f["core"] == p, 0, 1)
        cut = slice(p * half, (p + 1) * half)

        def left(q):
            return jnp.where(part == 0, mine[(q, *at)], sib[(q, *at)])

        m0, m1 = left(0), left(1)

        @pl.when(f["j"] == f["c"][0])
        def _():
            new[cut, :] = m0

        @pl.when(f["j"] == f["c"][1])
        def _():
            new[cut, :] = m1

        @pl.when(jnp.logical_and(f["j"] != f["c"][0], f["j"] != f["c"][1]))
        def _():
            w = (old[cut, :].astype(jnp.float32) - dot(m0, upper[0])).astype(new.dtype)
            w = w.astype(jnp.float32) - dot(m1, upper[1])
            new[cut, :] = w.astype(new.dtype)


def finish(n, m, piv, upper, lefts, mine, sib, raw, moved, out, old, new, sems):
    rb = raw.shape[0]
    f = facts(n, m, rb, piv)
    copies = []
    for k in range(rb - 1):
        update(f, upper, mine, sib, (k,), raw.at[k], new.at[k])
        copies.append(pltpu.make_async_copy(new.at[k], out.at[f["slots"][k]], sems.at[k]))
        copies[-1].start()
    k = rb - 1
    low_first = f["low_first"]
    first = jnp.where(low_first, f["is_low"], f["is_high"])
    second = jnp.where(low_first, f["is_high"], f["is_low"])

    @pl.when(first)
    def _():
        new[k] = upper[0]

    @pl.when(second)
    def _():
        either(f["j"] == f["c"][0], new.at[k], lambda: lefts[...], lambda: upper[1])

    @pl.when(jnp.logical_not(jnp.logical_or(first, second)))
    def _():
        either(f["is_end"], old, lambda: moved[...], lambda: raw[k])
        update(f, upper, mine, sib, (k,), old, new.at[k])

    copies.append(pltpu.make_async_copy(new.at[k], out.at[f["slots"][k]], sems.at[k]))
    copies[-1].start()
    for copy in copies:
        copy.wait()


def local(matrix, pattern, inverses, pivots):
    n = lax.axis_size("prow")
    m = lax.axis_size("pcol")
    rb, width = matrix.shape[0], matrix.shape[1]
    half = width // 2
    chips = m // 2
    stages = chips.bit_length() - 1
    dt = matrix.dtype
    blocks = matrix.reshape(rb, width, width)

    def call(kernel, shapes, specs, *operands, scratch=(), aliases=(), products=0, place=VMEM, after=(), name=None, weight=0):
        outs = [jax.ShapeDtypeStruct(s, dt) for s in shapes]
        count = len(operands)
        scratch = [pltpu.VMEM(s, dt) if isinstance(s, tuple) else s for s in scratch]

        def body(*refs):
            kernel(n, m, *refs[:count], *refs[count + len(after) :])

        kinds = {"s": SMEM, "v": VMEM, "a": ANY}
        specs = [kinds[k] for k in specs.ljust(count, "v")] + [ANY] * len(after)
        result = pl.pallas_call(
            body,
            out_shape=outs,
            in_specs=specs,
            out_specs=[place] * len(outs),
            scratch_shapes=scratch,
            input_output_aliases=dict(aliases),
            compiler_params=GRANT,
            name=name or kernel.__name__,
            cost_estimate=pl.CostEstimate(
                flops=int(products * 2 * width**3),
                bytes_accessed=weight + sum(a.size * a.dtype.itemsize for a in operands),
                transcendentals=0,
            ),
        )(*operands, *after)
        return result if len(result) > 1 else result[0]

    def along(name, pairs, value):
        with jax.named_scope(name):
            return lax.ppermute(value, "prow", pairs)

    def sibling(name, value):
        with jax.named_scope(name):
            return lax.ppermute(value, "pcol", [(i, i ^ 1) for i in range(m)])

    def across(name, stage, value):
        pairs = []
        for i in range(m):
            bit = stage if i % 2 == 0 else stages - 1 - stage
            pairs.append((i, i ^ (2 << bit)))
        with jax.named_scope(name):
            return lax.ppermute(value, "pcol", pairs)

    def cross(name, s, values):
        return [across(name + str(s) + "ab"[i], s, v) for i, v in enumerate(values)]

    def passing(name, kernel, values, got, after=()):
        for s in range(stages - 1):
            step = lambda _n, _m, *refs: kernel(n, m, s, stages, *refs)
            shapes = [v.shape for v in values]
            values = call(
                step, shapes, "s", pivots, *values, *got, after=after, name="pass_" + name
            )
            values = [values] if len(shapes) == 1 else list(values)
            got = cross(name, s + 1, values)
        return [*values, *got]

    square, strip = (width, width), (half, width)
    raw, leaving, other = call(
        prepare,
        [(rb, *square), square, (rb, *strip)],
        "ss",
        pivots,
        pattern.T,
        blocks,
    )
    early = sibling("sib_early", other)
    exchange = [(0, n // 2), (n - 1, n // 2 - 1), (n // 2, 0), (n // 2 - 1, n - 1)]
    moved = along("swap", exchange, leaving)

    def split(stride):
        pairs = []
        for i in range(0, n, 2 * stride):
            pairs += [(i, i + stride), (n - 1 - i, n - 1 - i - stride)]
        return pairs

    extra = call(pick_extra, [strip], "s", pivots, raw, early)
    panel = call(pick, [(rb - 1, *strip)] * 2, "s", pivots, raw, early, after=[extra])
    got_extra = cross("extra", 0, [extra])
    got_stays = cross("stays", 0, panel)
    had, got = passing("extra", forward_extra, [extra], got_extra, after=[panel[0]])
    hand = lambda stride: lambda _n, _m, *refs: hand_on(n, m, stride, *refs)
    step = lambda _n, _m, *refs: forward_extra(n, m, stages - 1, stages, *refs)
    extra_here = call(step, [strip], "s", pivots, had, got, name="extra_here")
    stays = passing("stays", forward, panel, got_stays, after=[extra_here])

    step = lambda _n, _m, *refs: relay(n, m, n // 2, *refs)
    other_moved, send = call(
        step, [strip, square], "", leaving, moved, name="relay", after=[stays[0]]
    )
    sib_moved = sibling("sib_moved", other_moved)
    third = call(
        pick_third, [(2, 1, *strip)], "s", pivots, raw, early, moved, sib_moved, after=stays[2:]
    )
    got_third = cross("third", 0, [third])

    arrived = [leaving, moved]
    stride = n // 4
    while stride:
        got = along("row" + str(stride), split(stride), send)
        arrived.append(got)
        if stride > 1:
            send = call(hand(stride), [square], "", send, got, name="hand_on_row")
        stride //= 2

    came = [extra_here]
    send = extra_here
    stride = n // 2
    while stride:
        got = along("extra_z" + str(stride), split(stride), send)
        came.append(got)
        if stride > 1:
            send = call(hand(stride), [strip], "", send, got, name="hand_on", after=[third])
        stride //= 2
    third = passing("third", forward, [third], got_third, after=[send])
    vl = call(
        settle_extra,
        [(2, *strip)],
        "s",
        pivots,
        inverses,
        *came,
        products=0.5,
        after=[third[0], arrived[2]],
    )
    sib_vl = sibling("sib_vl", vl)
    step = lambda _n, _m, *refs: multiply(n, m, stages, *refs)
    mine = call(
        step,
        [(2, rb, *strip)],
        "s",
        pivots,
        inverses,
        vl,
        sib_vl,
        *stays,
        *third,
        scratch=[square],
        products=3 * rb / 2,
        name="multiply",
    )
    sib_mine = sibling("sib_mine", mine)
    upper, lefts = call(
        settle_rows,
        [(2, *square), square],
        "s",
        pivots,
        vl,
        sib_vl,
        *arrived,
        products=1,
        after=[mine],
    )
    result = call(
        finish,
        [blocks.shape],
        "s",
        pivots,
        upper,
        lefts,
        mine,
        sib_mine,
        raw,
        moved,
        scratch=[square, (rb, *square), pltpu.SemaphoreType.DMA((rb,))],
        products=2 * rb,
        place=ANY,
    )
    return result.reshape(matrix.shape)


def solution(mesh):
    placed = (P(None, "prow", None, "pcol"), P(), P(), P())
    return jax.shard_map(
        local, mesh=mesh, in_specs=placed, out_specs=P(None, "prow", None, "pcol"), check_vma=False
    )
```

```python
import functools

import jax
import jax.numpy as jnp
from jax import lax
from jax.experimental import pallas as pl
from jax.experimental.pallas import tpu as pltpu
from jax.sharding import PartitionSpec as P

SMEM = pl.BlockSpec(memory_space=pltpu.SMEM)
VMEM = pl.BlockSpec(memory_space=pltpu.VMEM)
ANY = pl.BlockSpec(memory_space=pl.ANY)
GRANT = pltpu.CompilerParams(vmem_limit_bytes=24 * 2**20)


def facts(n, m, rb, pivots):
    f = {}
    r = f["r"] = lax.axis_index("prow").astype(jnp.int32)
    j = f["j"] = lax.axis_index("pcol").astype(jnp.int32)
    f["core"] = j & 1
    f["chip"] = j >> 1
    low_first = f["low_first"] = pivots[0, 1] == 0
    shift = n.bit_length() - 1
    a_low = jnp.where(low_first, pivots[0, 0], pivots[1, 0]) >> shift
    a_high = jnp.where(low_first, pivots[1, 0], pivots[0, 0]) >> shift
    f["c"] = [pivots[0, 2], pivots[1, 2]]
    is_low, is_high = r == n // 2, r == n // 2 - 1
    f["is_low"], f["is_high"] = is_low, is_high
    f["is_end"] = jnp.logical_or(r == 0, r == n - 1)
    out = jnp.where(is_low, a_low, jnp.where(is_high, a_high, jnp.where(r == 0, 0, rb - 1)))
    f["slots"] = []
    for k in range(rb):
        slot = out + (1 + k)
        f["slots"].append(jnp.where(slot >= rb, slot - rb, slot))
    f["cx"] = jnp.where((r == 0) == low_first, pivots[1, 2], pivots[0, 2])
    return f


def either(cond, out_ref, yes, no):
    @pl.when(cond)
    def _():
        out_ref[...] = yes()

    @pl.when(jnp.logical_not(cond))
    def _():
        out_ref[...] = no()


def rows(part, half):
    return pl.ds(pl.multiple_of(part * half, half), half)


def prepare(n, m, piv, pat, mat, raw, leaving, other):
    rb, width = mat.shape[0], mat.shape[1]
    f = facts(n, m, rb, piv)
    cut = rows(1 - f["core"], width // 2)
    for k in reversed(range(rb)):
        slot = f["slots"][k]
        keep = pat[f["j"], slot * n + f["r"]] != 0
        zero = lambda: jnp.zeros((width, width), mat.dtype)
        either(keep, raw.at[k], lambda: mat[slot], zero)
        if k == rb - 1:
            leaving[...] = raw[k]
        other[k] = raw[k, cut, :]


def views(refs, rb):
    if len(refs) == 2:
        refs = [refs[0].at[k] for k in range(rb)] + [refs[1].at[k] for k in range(rb - 1)]
    return refs[0], refs[1:rb], refs[rb:]


def pick(n, m, piv, raw, sib, *pieces):
    rb, width = raw.shape[0], raw.shape[1]
    f = facts(n, m, rb, piv)
    cut = rows(f["core"], width // 2)
    extra, *panel = views(pieces, rb)
    hit = (f["cx"] & 1) == f["core"]
    either(hit, extra, lambda: raw[rb - 1, cut, :], lambda: sib[rb - 1])
    for q in range(2):
        hit = (f["c"][q] & 1) == f["core"]
        for k in range(rb - 1):
            either(hit, panel[q][k], lambda: raw[k, cut, :], lambda: sib[k])


def pick_third(n, m, piv, raw, sib, moved, sib_moved, panel):
    rb, width = raw.shape[0], raw.shape[1]
    f = facts(n, m, rb, piv)
    cut = rows(f["core"], width // 2)
    for q in range(2):
        hit = (f["c"][q] & 1) == f["core"]

        @pl.when(f["is_end"])
        def _():
            either(hit, panel.at[q, 0], lambda: moved[cut, :], lambda: sib_moved[...])

        @pl.when(jnp.logical_not(f["is_end"]))
        def _():
            either(hit, panel.at[q, 0], lambda: raw[rb - 1, cut, :], lambda: sib[rb - 1])


def relay(n, m, stride, leaving, moved, other, send):
    core = lax.axis_index("pcol").astype(jnp.int32) & 1
    other[...] = moved[rows(1 - core, moved.shape[0] // 2), :]
    hand_on(n, m, stride, leaving, moved, send)


def bit_of(f, column, stage, stages):
    apart = f["chip"] ^ (column >> 1)
    bit = jnp.where(f["core"] == 0, stage, stages - 1 - stage)
    return ((apart >> bit) & 1) == 1


def forward_extra(n, m, stage, stages, piv, had, got, out):
    f = facts(n, m, 2, piv)
    take = bit_of(f, f["cx"], stage, stages)
    either(take, out, lambda: got[0], lambda: had[0])


def forward(n, m, stage, stages, piv, had, got, out):
    f = facts(n, m, 2, piv)
    for q in range(2):
        take = bit_of(f, f["c"][q], stage, stages)
        either(take, out.at[q], lambda: got[q], lambda: had[q])


def forward_all(n, m, rb, stage, stages, piv, *refs):
    f = facts(n, m, 2, piv)
    count = (len(refs) - 2) // 2
    had, got = views(refs[:count], rb), views(refs[count:-2], rb)
    out = views(refs[-2:], rb)
    take = bit_of(f, f["cx"], stage, stages)
    either(take, out[0], lambda: got[0][...], lambda: had[0][...])
    for q in range(2):
        take = bit_of(f, f["c"][q], stage, stages)
        for k in range(rb - 1):
            either(take, out[1 + q][k], lambda: got[1 + q][k][...], lambda: had[1 + q][k][...])


def hand_on(n, m, stride, had, got, extra):
    r = lax.axis_index("prow").astype(jnp.int32)
    low = (r & (2 * stride - 1)) == stride
    high = ((n - 1 - r) & (2 * stride - 1)) == stride
    either(jnp.logical_or(low, high), extra, lambda: got[...], lambda: had[...])


def dot(left, right):
    return jnp.dot(left, right, preferred_element_type=jnp.float32)


def settle_extra(n, m, piv, inv, *refs):
    had, out = refs[:-1], refs[-1]
    f = facts(n, m, 2, piv)
    r = f["r"]
    stages = len(had) - 1
    for which in range(2):
        place = r if which == 0 else n - 1 - r
        low_is_v = f["low_first"] if which == 0 else jnp.logical_not(f["low_first"])
        for s in range(stages + 1):
            if s == 0:
                here = place == 0
            else:
                here = (place & (2 * (n >> s) - 1)) == (n >> s)

            @pl.when(jnp.logical_and(here, low_is_v))
            def _():
                out[0] = had[s][...]

            @pl.when(jnp.logical_and(here, jnp.logical_not(low_is_v)))
            def _():
                out[1] = had[s][...]

    out[1] = dot(out[1], inv[0]).astype(out.dtype)


def multiply(n, m, stages, piv, inv, vl, sib_vl, *refs):
    panels, third, third_got, out, v = refs[:-4], refs[-4], refs[-3], refs[-2], refs[-1]
    f = facts(n, m, 2, piv)
    half = vl.shape[1]
    v[rows(f["core"], half), :] = vl[0]
    v[rows(1 - f["core"], half), :] = sib_vl[0]
    count = out.shape[1] - 1
    for q in range(2):
        take = bit_of(f, f["c"][q], stages - 1, stages)
        had, got = (views(panels[i : i + 2], count + 1)[1 + q] for i in (0, 2))
        for k in range(count):
            either(take, out.at[q, k], lambda: got[k][...], lambda: had[k][...])
        either(take, out.at[q, count], lambda: third_got[q, 0], lambda: third[q, 0])
    for k in range(count + 1):
        m0 = dot(out[0, k], inv[0]).astype(out.dtype)
        p1 = (out[1, k].astype(jnp.float32) - dot(m0, v[...])).astype(out.dtype)
        out[0, k] = m0
        out[1, k] = dot(p1, inv[1]).astype(out.dtype)


def settle_rows(n, m, piv, vl, sib_vl, *refs):
    came, upper, lefts = refs[:-2], refs[-2], refs[-1]
    half = came[0].shape[0] // 2
    f = facts(n, m, 2, piv)
    r = f["r"]
    for which in range(2):
        place = r if which == 0 else n - 1 - r
        slot = jnp.where(f["low_first"], which, 1 - which)
        for s in range(len(came)):
            here = place == 0 if s == 0 else (place & (2 * (n >> s) - 1)) == (n >> s)

            @pl.when(here)
            def _():
                upper[slot] = came[s][...]

    lefts[rows(f["core"], half), :] = vl[1]
    lefts[rows(1 - f["core"], half), :] = sib_vl[1]
    for p in range(2):
        cut = slice(p * half, (p + 1) * half)
        fresh = upper[1, cut, :].astype(jnp.float32) - dot(lefts[cut, :], upper[0])
        upper[1, cut, :] = fresh.astype(upper.dtype)


def update(f, upper, mine, sib, at, old, new):
    half = old.shape[0] // 2
    for p in range(2):
        part = jnp.where(f["core"] == p, 0, 1)
        cut = slice(p * half, (p + 1) * half)

        def left(q):
            return jnp.where(part == 0, mine[(q, *at)], sib[(q, *at)])

        m0, m1 = left(0), left(1)

        @pl.when(f["j"] == f["c"][0])
        def _():
            new[cut, :] = m0

        @pl.when(f["j"] == f["c"][1])
        def _():
            new[cut, :] = m1

        @pl.when(jnp.logical_and(f["j"] != f["c"][0], f["j"] != f["c"][1]))
        def _():
            w = (old[cut, :].astype(jnp.float32) - dot(m0, upper[0])).astype(new.dtype)
            w = w.astype(jnp.float32) - dot(m1, upper[1])
            new[cut, :] = w.astype(new.dtype)


def finish(n, m, piv, upper, lefts, mine, sib, raw, moved, out, old, new, sems):
    rb = raw.shape[0]
    f = facts(n, m, rb, piv)
    copies = []
    for k in range(rb - 1):
        update(f, upper, mine, sib, (k,), raw.at[k], new.at[k])
        copies.append(pltpu.make_async_copy(new.at[k], out.at[f["slots"][k]], sems.at[k]))
        copies[-1].start()
    k = rb - 1
    low_first = f["low_first"]
    first = jnp.where(low_first, f["is_low"], f["is_high"])
    second = jnp.where(low_first, f["is_high"], f["is_low"])

    @pl.when(first)
    def _():
        new[k] = upper[0]

    @pl.when(second)
    def _():
        either(f["j"] == f["c"][0], new.at[k], lambda: lefts[...], lambda: upper[1])

    @pl.when(jnp.logical_not(jnp.logical_or(first, second)))
    def _():
        either(f["is_end"], old, lambda: moved[...], lambda: raw[k])
        update(f, upper, mine, sib, (k,), old, new.at[k])

    copies.append(pltpu.make_async_copy(new.at[k], out.at[f["slots"][k]], sems.at[k]))
    copies[-1].start()
    for copy in copies:
        copy.wait()


def local(matrix, pattern, inverses, pivots):
    n = lax.axis_size("prow")
    m = lax.axis_size("pcol")
    rb, width = matrix.shape[0], matrix.shape[1]
    half = width // 2
    chips = m // 2
    stages = chips.bit_length() - 1
    dt = matrix.dtype
    blocks = matrix.reshape(rb, width, width)

    def call(kernel, shapes, specs, *operands, scratch=(), aliases=(), products=0, place=VMEM, after=(), name=None, weight=0):
        outs = [jax.ShapeDtypeStruct(s, dt) for s in shapes]
        count = len(operands)
        scratch = [pltpu.VMEM(s, dt) if isinstance(s, tuple) else s for s in scratch]

        def body(*refs):
            kernel(n, m, *refs[:count], *refs[count + len(after) :])

        kinds = {"s": SMEM, "v": VMEM, "a": ANY}
        specs = [kinds[k] for k in specs.ljust(count, "v")] + [ANY] * len(after)
        result = pl.pallas_call(
            body,
            out_shape=outs,
            in_specs=specs,
            out_specs=[place] * len(outs),
            scratch_shapes=scratch,
            input_output_aliases=dict(aliases),
            compiler_params=GRANT,
            name=name or kernel.__name__,
            cost_estimate=pl.CostEstimate(
                flops=int(products * 2 * width**3),
                bytes_accessed=weight + sum(a.size * a.dtype.itemsize for a in operands),
                transcendentals=0,
            ),
        )(*operands, *after)
        return result if len(result) > 1 else result[0]

    def along(name, pairs, value):
        with jax.named_scope(name):
            return lax.ppermute(value, "prow", pairs)

    def sibling(name, value):
        with jax.named_scope(name):
            return lax.ppermute(value, "pcol", [(i, i ^ 1) for i in range(m)])

    def across(name, stage, value):
        pairs = []
        for i in range(m):
            bit = stage if i % 2 == 0 else stages - 1 - stage
            pairs.append((i, i ^ (2 << bit)))
        with jax.named_scope(name):
            return lax.ppermute(value, "pcol", pairs)

    square, strip = (width, width), (half, width)
    raw, leaving, other = call(
        prepare,
        [(rb, *square), square, (rb, *strip)],
        "ss",
        pivots,
        pattern.T,
        blocks,
    )
    early = sibling("sib_early", other)
    exchange = [(0, n // 2), (n - 1, n // 2 - 1), (n // 2, 0), (n // 2 - 1, n - 1)]
    moved = along("swap", exchange, leaving)

    def split(stride):
        pairs = []
        for i in range(0, n, 2 * stride):
            pairs += [(i, i + stride), (n - 1 - i, n - 1 - i - stride)]
        return pairs

    hand = lambda stride: lambda _n, _m, *refs: hand_on(n, m, stride, *refs)
    panel = call(pick, [strip] * (2 * rb - 1), "s", pivots, raw, early)
    got = [across("stays0", 0, piece) for piece in panel]
    for s in range(stages - 1):
        step = lambda _n, _m, *refs: forward_all(n, m, rb, s, stages, *refs)
        panel = call(
            step, [(rb, *strip), (rb - 1, *strip)], "s", pivots, *panel, *got, name="forward_all"
        )
        got = [across("stays" + str(s + 1), s + 1, part) for part in panel]

    step = lambda _n, _m, *refs: forward_extra(n, m, stages - 1, stages, *refs)
    extra_here = call(
        step, [strip], "s", pivots, panel[0], got[0], name="extra_here"
    )

    step = lambda _n, _m, *refs: relay(n, m, n // 2, *refs)
    other_moved, send = call(
        step, [strip, square], "", leaving, moved, name="relay", after=[extra_here]
    )
    sib_moved = sibling("sib_moved", other_moved)
    stays = [*panel, *got]
    arrived = [leaving, moved]
    stride = n // 4
    while stride:
        got = along("row" + str(stride), split(stride), send)
        arrived.append(got)
        if stride > 1:
            send = call(hand(stride), [square], "", send, got, name="hand_on_row")
        stride //= 2

    came = [extra_here]
    send = extra_here
    stride = n // 2
    while stride:
        got = along("extra_z" + str(stride), split(stride), send)
        came.append(got)
        if stride > 1:
            send = call(hand(stride), [strip], "", send, got, name="hand_on", after=[other_moved])
        stride //= 2
    third = call(
        pick_third,
        [(2, 1, *strip)],
        "s",
        pivots,
        raw,
        early,
        moved,
        sib_moved,
        after=[send, stays[-1]],
    )
    third_got = across("third0", 0, third)
    for s in range(stages - 1):
        step = lambda _n, _m, *refs: forward(n, m, s, stages, *refs)
        third = call(
            step, [third.shape], "s", pivots, third, third_got, name="forward_third"
        )
        third_got = across("third" + str(s + 1), s + 1, third)
    vl = call(
        settle_extra,
        [(2, *strip)],
        "s",
        pivots,
        inverses,
        *came,
        products=0.5,
        after=[third, arrived[2]],
    )
    sib_vl = sibling("sib_vl", vl)
    step = lambda _n, _m, *refs: multiply(n, m, stages, *refs)
    mine = call(
        step,
        [(2, rb, *strip)],
        "s",
        pivots,
        inverses,
        vl,
        sib_vl,
        *stays,
        third,
        third_got,
        scratch=[square],
        products=3 * rb / 2,
        name="multiply",
    )
    sib_mine = sibling("sib_mine", mine)
    upper, lefts = call(
        settle_rows,
        [(2, *square), square],
        "s",
        pivots,
        vl,
        sib_vl,
        *arrived,
        products=1,
        after=[mine],
    )
    result = call(
        finish,
        [blocks.shape],
        "s",
        pivots,
        upper,
        lefts,
        mine,
        sib_mine,
        raw,
        moved,
        scratch=[square, (rb, *square), pltpu.SemaphoreType.DMA((rb,))],
        products=2 * rb,
        place=ANY,
    )
    return result.reshape(matrix.shape)


def solution(mesh):
    placed = (P(None, "prow", None, "pcol"), P(), P(), P())
    return jax.shard_map(
        local, mesh=mesh, in_specs=placed, out_specs=P(None, "prow", None, "pcol"), check_vma=False
    )
```

```python
import functools

import jax
import jax.numpy as jnp
from jax import lax
from jax.experimental import pallas as pl
from jax.experimental.pallas import tpu as pltpu
from jax.sharding import PartitionSpec as P

SMEM = pl.BlockSpec(memory_space=pltpu.SMEM)
VMEM = pl.BlockSpec(memory_space=pltpu.VMEM)
ANY = pl.BlockSpec(memory_space=pl.ANY)
GRANT = pltpu.CompilerParams(vmem_limit_bytes=24 * 2**20)


def facts(n, m, rb, pivots):
    f = {}
    r = f["r"] = lax.axis_index("prow").astype(jnp.int32)
    j = f["j"] = lax.axis_index("pcol").astype(jnp.int32)
    f["core"] = j & 1
    f["chip"] = j >> 1
    low_first = f["low_first"] = pivots[0, 1] == 0
    shift = n.bit_length() - 1
    a_low = jnp.where(low_first, pivots[0, 0], pivots[1, 0]) >> shift
    a_high = jnp.where(low_first, pivots[1, 0], pivots[0, 0]) >> shift
    f["c"] = [pivots[0, 2], pivots[1, 2]]
    is_low, is_high = r == n // 2, r == n // 2 - 1
    f["is_low"], f["is_high"] = is_low, is_high
    f["is_end"] = jnp.logical_or(r == 0, r == n - 1)
    out = jnp.where(is_low, a_low, jnp.where(is_high, a_high, jnp.where(r == 0, 0, rb - 1)))
    f["slots"] = []
    for k in range(rb):
        slot = out + (1 + k)
        f["slots"].append(jnp.where(slot >= rb, slot - rb, slot))
    f["cx"] = jnp.where((r == 0) == low_first, pivots[1, 2], pivots[0, 2])
    return f


def either(cond, out_ref, yes, no):
    @pl.when(cond)
    def _():
        out_ref[...] = yes()

    @pl.when(jnp.logical_not(cond))
    def _():
        out_ref[...] = no()


def rows(part, half):
    return pl.ds(pl.multiple_of(part * half, half), half)


def prepare(n, m, piv, pat, mat, raw, leaving, other):
    rb, width = mat.shape[0], mat.shape[1]
    f = facts(n, m, rb, piv)
    cut = rows(1 - f["core"], width // 2)
    for k in reversed(range(rb)):
        slot = f["slots"][k]
        keep = pat[f["j"], slot * n + f["r"]] != 0
        zero = lambda: jnp.zeros((width, width), mat.dtype)
        either(keep, raw.at[k], lambda: mat[slot], zero)
        if k == rb - 1:
            leaving[...] = raw[k]
        other[k] = raw[k, cut, :]


def views(refs, rb):
    if len(refs) == 2:
        refs = [refs[0].at[k] for k in range(rb)] + [refs[1].at[k] for k in range(rb - 1)]
    return refs[0], refs[1:rb], refs[rb:]


def pick(n, m, piv, raw, sib, *pieces):
    rb, width = raw.shape[0], raw.shape[1]
    f = facts(n, m, rb, piv)
    cut = rows(f["core"], width // 2)
    extra, *panel = views(pieces, rb)
    hit = (f["cx"] & 1) == f["core"]
    either(hit, extra, lambda: raw[rb - 1, cut, :], lambda: sib[rb - 1])
    for q in range(2):
        hit = (f["c"][q] & 1) == f["core"]
        for k in range(rb - 1):
            either(hit, panel[q][k], lambda: raw[k, cut, :], lambda: sib[k])


def pick_third(n, m, piv, raw, sib, moved, sib_moved, panel):
    rb, width = raw.shape[0], raw.shape[1]
    f = facts(n, m, rb, piv)
    cut = rows(f["core"], width // 2)
    for q in range(2):
        hit = (f["c"][q] & 1) == f["core"]

        @pl.when(f["is_end"])
        def _():
            either(hit, panel.at[q, 0], lambda: moved[cut, :], lambda: sib_moved[...])

        @pl.when(jnp.logical_not(f["is_end"]))
        def _():
            either(hit, panel.at[q, 0], lambda: raw[rb - 1, cut, :], lambda: sib[rb - 1])


def relay(n, m, stride, leaving, moved, other, send):
    core = lax.axis_index("pcol").astype(jnp.int32) & 1
    other[...] = moved[rows(1 - core, moved.shape[0] // 2), :]
    hand_on(n, m, stride, leaving, moved, send)


def bit_of(f, column, stage, stages):
    apart = f["chip"] ^ (column >> 1)
    bit = jnp.where(f["core"] == 0, stage, stages - 1 - stage)
    return ((apart >> bit) & 1) == 1


def forward_extra(n, m, stage, stages, piv, had, got, out):
    f = facts(n, m, 2, piv)
    take = bit_of(f, f["cx"], stage, stages)
    either(take, out, lambda: got[0], lambda: had[0])


def forward(n, m, stage, stages, piv, had, got, out):
    f = facts(n, m, 2, piv)
    for q in range(2):
        take = bit_of(f, f["c"][q], stage, stages)
        either(take, out.at[q], lambda: got[q], lambda: had[q])


def forward_all(n, m, rb, stage, stages, piv, *refs):
    f = facts(n, m, 2, piv)
    count = (len(refs) - 2) // 2
    had, got = views(refs[:count], rb), views(refs[count:-2], rb)
    out = views(refs[-2:], rb)
    take = bit_of(f, f["cx"], stage, stages)
    either(take, out[0], lambda: got[0][...], lambda: had[0][...])
    for q in range(2):
        take = bit_of(f, f["c"][q], stage, stages)
        for k in range(rb - 1):
            either(take, out[1 + q][k], lambda: got[1 + q][k][...], lambda: had[1 + q][k][...])


def hand_on(n, m, stride, had, got, extra):
    r = lax.axis_index("prow").astype(jnp.int32)
    low = (r & (2 * stride - 1)) == stride
    high = ((n - 1 - r) & (2 * stride - 1)) == stride
    either(jnp.logical_or(low, high), extra, lambda: got[...], lambda: had[...])


def dot(left, right):
    return jnp.dot(left, right, preferred_element_type=jnp.float32)


def settle_extra(n, m, piv, inv, *refs):
    had, out = refs[:-2], refs[-2:]
    f = facts(n, m, 2, piv)
    r = f["r"]
    stages = len(had) - 1
    for which in range(2):
        place = r if which == 0 else n - 1 - r
        low_is_v = f["low_first"] if which == 0 else jnp.logical_not(f["low_first"])
        for s in range(stages + 1):
            if s == 0:
                here = place == 0
            else:
                here = (place & (2 * (n >> s) - 1)) == (n >> s)

            @pl.when(jnp.logical_and(here, low_is_v))
            def _():
                out[0][...] = had[s][...]

            @pl.when(jnp.logical_and(here, jnp.logical_not(low_is_v)))
            def _():
                out[1][...] = had[s][...]

    out[1][...] = dot(out[1][...], inv[0]).astype(out[1].dtype)


def multiply(n, m, stages, piv, inv, v_half, sib_v, *refs):
    panels, third, third_got, out, v = refs[:-4], refs[-4], refs[-3], refs[-2], refs[-1]
    f = facts(n, m, 2, piv)
    half = v_half.shape[0]
    v[rows(f["core"], half), :] = v_half[...]
    v[rows(1 - f["core"], half), :] = sib_v[...]
    count = out.shape[1] - 1
    for q in range(2):
        take = bit_of(f, f["c"][q], stages - 1, stages)
        had, got = (views(panels[i : i + 2], count + 1)[1 + q] for i in (0, 2))
        for k in range(count):
            either(take, out.at[q, k], lambda: got[k][...], lambda: had[k][...])
        either(take, out.at[q, count], lambda: third_got[q, 0], lambda: third[q, 0])
    for k in range(count + 1):
        m0 = dot(out[0, k], inv[0]).astype(out.dtype)
        p1 = (out[1, k].astype(jnp.float32) - dot(m0, v[...])).astype(out.dtype)
        out[0, k] = m0
        out[1, k] = dot(p1, inv[1]).astype(out.dtype)


def settle_rows(n, m, piv, l_half, sib_l, *refs):
    came, upper, lefts = refs[:-2], refs[-2], refs[-1]
    half = came[0].shape[0] // 2
    f = facts(n, m, 2, piv)
    r = f["r"]
    for which in range(2):
        place = r if which == 0 else n - 1 - r
        slot = jnp.where(f["low_first"], which, 1 - which)
        for s in range(len(came)):
            here = place == 0 if s == 0 else (place & (2 * (n >> s) - 1)) == (n >> s)

            @pl.when(here)
            def _():
                upper[slot] = came[s][...]

    lefts[rows(f["core"], half), :] = l_half[...]
    lefts[rows(1 - f["core"], half), :] = sib_l[...]
    for p in range(2):
        cut = slice(p * half, (p + 1) * half)
        fresh = upper[1, cut, :].astype(jnp.float32) - dot(lefts[cut, :], upper[0])
        upper[1, cut, :] = fresh.astype(upper.dtype)


def update(f, upper, mine, sib, at, old, new):
    half = old.shape[0] // 2
    for p in range(2):
        part = jnp.where(f["core"] == p, 0, 1)
        cut = slice(p * half, (p + 1) * half)

        def left(q):
            return jnp.where(part == 0, mine[(q, *at)], sib[(q, *at)])

        m0, m1 = left(0), left(1)

        @pl.when(f["j"] == f["c"][0])
        def _():
            new[cut, :] = m0

        @pl.when(f["j"] == f["c"][1])
        def _():
            new[cut, :] = m1

        @pl.when(jnp.logical_and(f["j"] != f["c"][0], f["j"] != f["c"][1]))
        def _():
            w = (old[cut, :].astype(jnp.float32) - dot(m0, upper[0])).astype(new.dtype)
            w = w.astype(jnp.float32) - dot(m1, upper[1])
            new[cut, :] = w.astype(new.dtype)


def finish(n, m, piv, upper, lefts, mine, sib, raw, moved, out, old, new, sems):
    rb = raw.shape[0]
    f = facts(n, m, rb, piv)
    copies = []
    for k in range(rb - 1):
        update(f, upper, mine, sib, (k,), raw.at[k], new.at[k])
        copies.append(pltpu.make_async_copy(new.at[k], out.at[f["slots"][k]], sems.at[k]))
        copies[-1].start()
    k = rb - 1
    low_first = f["low_first"]
    first = jnp.where(low_first, f["is_low"], f["is_high"])
    second = jnp.where(low_first, f["is_high"], f["is_low"])

    @pl.when(first)
    def _():
        new[k] = upper[0]

    @pl.when(second)
    def _():
        either(f["j"] == f["c"][0], new.at[k], lambda: lefts[...], lambda: upper[1])

    @pl.when(jnp.logical_not(jnp.logical_or(first, second)))
    def _():
        either(f["is_end"], old, lambda: moved[...], lambda: raw[k])
        update(f, upper, mine, sib, (k,), old, new.at[k])

    copies.append(pltpu.make_async_copy(new.at[k], out.at[f["slots"][k]], sems.at[k]))
    copies[-1].start()
    for copy in copies:
        copy.wait()


def local(matrix, pattern, inverses, pivots):
    n = lax.axis_size("prow")
    m = lax.axis_size("pcol")
    rb, width = matrix.shape[0], matrix.shape[1]
    half = width // 2
    chips = m // 2
    stages = chips.bit_length() - 1
    dt = matrix.dtype
    blocks = matrix.reshape(rb, width, width)

    def call(
        kernel, shapes, specs, *operands, scratch=(), products=0, place=VMEM, after=(), name=None
    ):
        outs = [jax.ShapeDtypeStruct(s, dt) for s in shapes]
        count = len(operands)
        scratch = [pltpu.VMEM(s, dt) if isinstance(s, tuple) else s for s in scratch]

        def body(*refs):
            kernel(n, m, *refs[:count], *refs[count + len(after) :])

        kinds = {"s": SMEM, "v": VMEM, "a": ANY}
        specs = [kinds[k] for k in specs.ljust(count, "v")] + [ANY] * len(after)
        result = pl.pallas_call(
            body,
            out_shape=outs,
            in_specs=specs,
            out_specs=[place] * len(outs),
            scratch_shapes=scratch,
            compiler_params=GRANT,
            name=name or kernel.__name__,
            cost_estimate=pl.CostEstimate(
                flops=int(products * 2 * width**3),
                bytes_accessed=sum(a.size * a.dtype.itemsize for a in operands),
                transcendentals=0,
            ),
        )(*operands, *after)
        return result if len(result) > 1 else result[0]

    def along(name, pairs, value):
        with jax.named_scope(name):
            return lax.ppermute(value, "prow", pairs)

    def sibling(name, value):
        with jax.named_scope(name):
            return lax.ppermute(value, "pcol", [(i, i ^ 1) for i in range(m)])

    def across(name, stage, value):
        pairs = []
        for i in range(m):
            bit = stage if i % 2 == 0 else stages - 1 - stage
            pairs.append((i, i ^ (2 << bit)))
        with jax.named_scope(name):
            return lax.ppermute(value, "pcol", pairs)

    square, strip = (width, width), (half, width)
    raw, leaving, other = call(
        prepare,
        [(rb, *square), square, (rb, *strip)],
        "ss",
        pivots,
        pattern.T,
        blocks,
    )
    early = sibling("sib_early", other)
    exchange = [(0, n // 2), (n - 1, n // 2 - 1), (n // 2, 0), (n // 2 - 1, n - 1)]
    moved = along("swap", exchange, leaving)

    def split(stride):
        pairs = []
        for i in range(0, n, 2 * stride):
            pairs += [(i, i + stride), (n - 1 - i, n - 1 - i - stride)]
        return pairs

    hand = lambda stride: lambda _n, _m, *refs: hand_on(n, m, stride, *refs)
    panel = call(pick, [strip] * (2 * rb - 1), "s", pivots, raw, early)
    got = [across("stays0", 0, piece) for piece in panel]
    step = lambda _n, _m, *refs: relay(n, m, n // 2, *refs)
    other_moved, send = call(
        step, [strip, square], "", leaving, moved, name="relay", after=got
    )
    for s in range(stages - 1):
        step = lambda _n, _m, *refs: forward_all(n, m, rb, s, stages, *refs)
        panel = call(
            step,
            [(rb, *strip), (rb - 1, *strip)],
            "s",
            pivots,
            *panel,
            *got,
            name="forward_all",
            after=[send],
        )
        got = [across("stays" + str(s + 1), s + 1, part) for part in panel]

    sib_moved = sibling("sib_moved", other_moved)
    step = lambda _n, _m, *refs: forward_extra(n, m, stages - 1, stages, *refs)
    extra_here = call(
        step, [strip], "s", pivots, panel[0], got[0], name="extra_here"
    )
    stays = [*panel, *got]
    third = call(
        pick_third,
        [(2, 1, *strip)],
        "s",
        pivots,
        raw,
        early,
        moved,
        sib_moved,
        after=[extra_here, stays[-1]],
    )
    third_got = across("third0", 0, third)

    arrived = [leaving, moved]
    stride = n // 4
    while stride:
        got = along("row" + str(stride), split(stride), send)
        arrived.append(got)
        if stride > 1:
            send = call(hand(stride), [square], "", send, got, name="hand_on_row")
        stride //= 2

    came = [extra_here]
    send = extra_here
    stride = n // 2
    while stride:
        got = along("extra_z" + str(stride), split(stride), send)
        came.append(got)
        if stride > 1:
            send = call(hand(stride), [strip], "", send, got, name="hand_on", after=[third])
        stride //= 2
    for s in range(stages - 1):
        step = lambda _n, _m, *refs: forward(n, m, s, stages, *refs)
        third = call(
            step, [third.shape], "s", pivots, third, third_got, name="forward_third"
        )
        third_got = across("third" + str(s + 1), s + 1, third)
    v_half, l_half = call(
        settle_extra,
        [strip] * 2,
        "s",
        pivots,
        inverses,
        *came,
        products=0.5,
        after=[third, arrived[2]],
    )
    sib_v = sibling("sib_v", v_half)
    sib_l = sibling("sib_l", l_half)
    step = lambda _n, _m, *refs: multiply(n, m, stages, *refs)
    mine = call(
        step,
        [(2, rb, *strip)],
        "s",
        pivots,
        inverses,
        v_half,
        sib_v,
        *stays,
        third,
        third_got,
        scratch=[square],
        products=3 * rb / 2,
        name="multiply",
        after=[sib_l],
    )
    sib_mine = sibling("sib_mine", mine)
    upper, lefts = call(
        settle_rows,
        [(2, *square), square],
        "s",
        pivots,
        l_half,
        sib_l,
        *arrived,
        products=1,
        after=[mine],
    )
    result = call(
        finish,
        [blocks.shape],
        "s",
        pivots,
        upper,
        lefts,
        mine,
        sib_mine,
        raw,
        moved,
        scratch=[square, (rb, *square), pltpu.SemaphoreType.DMA((rb,))],
        products=2 * rb,
        place=ANY,
    )
    return result.reshape(matrix.shape)


def solution(mesh):
    placed = (P(None, "prow", None, "pcol"), P(), P(), P())
    return jax.shard_map(
        local, mesh=mesh, in_specs=placed, out_specs=P(None, "prow", None, "pcol"), check_vma=False
    )
```

```python
import functools

import jax
import jax.numpy as jnp
from jax import lax
from jax.experimental import pallas as pl
from jax.experimental.pallas import tpu as pltpu
from jax.sharding import PartitionSpec as P

SMEM = pl.BlockSpec(memory_space=pltpu.SMEM)
VMEM = pl.BlockSpec(memory_space=pltpu.VMEM)
ANY = pl.BlockSpec(memory_space=pl.ANY)
GRANT = pltpu.CompilerParams(vmem_limit_bytes=24 * 2**20)


def facts(n, m, rb, pivots):
    f = {}
    r = f["r"] = lax.axis_index("prow").astype(jnp.int32)
    j = f["j"] = lax.axis_index("pcol").astype(jnp.int32)
    f["core"] = j & 1
    f["chip"] = j >> 1
    low_first = f["low_first"] = pivots[0, 1] == 0
    shift = n.bit_length() - 1
    a_low = jnp.where(low_first, pivots[0, 0], pivots[1, 0]) >> shift
    a_high = jnp.where(low_first, pivots[1, 0], pivots[0, 0]) >> shift
    f["c"] = [pivots[0, 2], pivots[1, 2]]
    is_low, is_high = r == n // 2, r == n // 2 - 1
    f["is_low"], f["is_high"] = is_low, is_high
    f["is_end"] = jnp.logical_or(r == 0, r == n - 1)
    out = jnp.where(is_low, a_low, jnp.where(is_high, a_high, jnp.where(r == 0, 0, rb - 1)))
    f["slots"] = []
    for k in range(rb):
        slot = out + (1 + k)
        f["slots"].append(jnp.where(slot >= rb, slot - rb, slot))
    f["cx"] = jnp.where((r == 0) == low_first, pivots[1, 2], pivots[0, 2])
    return f


def either(cond, out_ref, yes, no):
    @pl.when(cond)
    def _():
        out_ref[...] = yes()

    @pl.when(jnp.logical_not(cond))
    def _():
        out_ref[...] = no()


def rows(part, half):
    return pl.ds(pl.multiple_of(part * half, half), half)


def prepare(n, m, piv, pat, mat, raw, leaving, other):
    rb, width = mat.shape[0], mat.shape[1]
    f = facts(n, m, rb, piv)
    cut = rows(1 - f["core"], width // 2)
    for k in reversed(range(rb)):
        slot = f["slots"][k]
        keep = pat[f["j"], slot * n + f["r"]] != 0
        zero = lambda: jnp.zeros((width, width), mat.dtype)
        either(keep, raw.at[k], lambda: mat[slot], zero)
        if k == rb - 1:
            leaving[...] = raw[k]
        other[k] = raw[k, cut, :]


def views(refs, rb):
    if refs[0].shape[0] == rb:
        one = [refs[0].at[k] for k in range(rb)] + [refs[1].at[k] for k in range(rb - 1)]
        return one[0], one[1:rb], one[rb:]
    one = [ref.at[0] for ref in refs]
    return refs[-1].at[1], one[: rb - 1], one[rb - 1 :]


def pick(n, m, piv, raw, sib, *pieces):
    rb, width = raw.shape[0], raw.shape[1]
    f = facts(n, m, rb, piv)
    cut = rows(f["core"], width // 2)
    extra, *panel = views(pieces, rb)
    hit = (f["cx"] & 1) == f["core"]
    either(hit, extra, lambda: raw[rb - 1, cut, :], lambda: sib[rb - 1])
    for q in range(2):
        hit = (f["c"][q] & 1) == f["core"]
        for k in range(rb - 1):
            either(hit, panel[q][k], lambda: raw[k, cut, :], lambda: sib[k])


def pick_third(n, m, piv, raw, sib, moved, sib_moved, panel):
    rb, width = raw.shape[0], raw.shape[1]
    f = facts(n, m, rb, piv)
    cut = rows(f["core"], width // 2)
    for q in range(2):
        hit = (f["c"][q] & 1) == f["core"]

        @pl.when(f["is_end"])
        def _():
            either(hit, panel.at[q, 0], lambda: moved[cut, :], lambda: sib_moved[...])

        @pl.when(jnp.logical_not(f["is_end"]))
        def _():
            either(hit, panel.at[q, 0], lambda: raw[rb - 1, cut, :], lambda: sib[rb - 1])


def relay(n, m, stride, leaving, moved, other, send):
    core = lax.axis_index("pcol").astype(jnp.int32) & 1
    other[...] = moved[rows(1 - core, moved.shape[0] // 2), :]
    hand_on(n, m, stride, leaving, moved, send)


def bit_of(f, column, stage, stages):
    apart = f["chip"] ^ (column >> 1)
    bit = jnp.where(f["core"] == 0, stage, stages - 1 - stage)
    return ((apart >> bit) & 1) == 1


def forward_extra(n, m, stage, stages, piv, had, got, out):
    f = facts(n, m, 2, piv)
    take = bit_of(f, f["cx"], stage, stages)
    either(take, out, lambda: got[0], lambda: had[0])


def forward(n, m, stage, stages, piv, had, got, out):
    f = facts(n, m, 2, piv)
    for q in range(2):
        take = bit_of(f, f["c"][q], stage, stages)
        either(take, out.at[q], lambda: got[q], lambda: had[q])


def forward_all(n, m, rb, stage, stages, piv, *refs):
    f = facts(n, m, 2, piv)
    count = (len(refs) - 2) // 2
    had, got = views(refs[:count], rb), views(refs[count:-2], rb)
    out = views(refs[-2:], rb)
    take = bit_of(f, f["cx"], stage, stages)
    either(take, out[0], lambda: got[0][...], lambda: had[0][...])
    for q in range(2):
        take = bit_of(f, f["c"][q], stage, stages)
        for k in range(rb - 1):
            either(take, out[1 + q][k], lambda: got[1 + q][k][...], lambda: had[1 + q][k][...])


def hand_on(n, m, stride, had, got, extra):
    r = lax.axis_index("prow").astype(jnp.int32)
    low = (r & (2 * stride - 1)) == stride
    high = ((n - 1 - r) & (2 * stride - 1)) == stride
    either(jnp.logical_or(low, high), extra, lambda: got[...], lambda: had[...])


def dot(left, right):
    return jnp.dot(left, right, preferred_element_type=jnp.float32)


def settle_extra(n, m, piv, inv, *refs):
    had, out = refs[:-2], refs[-2:]
    f = facts(n, m, 2, piv)
    r = f["r"]
    stages = len(had) - 1
    for which in range(2):
        place = r if which == 0 else n - 1 - r
        low_is_v = f["low_first"] if which == 0 else jnp.logical_not(f["low_first"])
        for s in range(stages + 1):
            if s == 0:
                here = place == 0
            else:
                here = (place & (2 * (n >> s) - 1)) == (n >> s)

            @pl.when(jnp.logical_and(here, low_is_v))
            def _():
                out[0][...] = had[s][...]

            @pl.when(jnp.logical_and(here, jnp.logical_not(low_is_v)))
            def _():
                out[1][...] = had[s][...]

    out[1][...] = dot(out[1][...], inv[0]).astype(out[1].dtype)


def multiply(n, m, stages, piv, inv, v_half, sib_v, *refs):
    panels, third, third_got, out, v = refs[:-4], refs[-4], refs[-3], refs[-2], refs[-1]
    f = facts(n, m, 2, piv)
    half = v_half.shape[0]
    v[rows(f["core"], half), :] = v_half[...]
    v[rows(1 - f["core"], half), :] = sib_v[...]
    count = out.shape[1] - 1
    for q in range(2):
        take = bit_of(f, f["c"][q], stages - 1, stages)
        had, got = (views(panels[i : i + 2], count + 1)[1 + q] for i in (0, 2))
        for k in range(count):
            either(take, out.at[q, k], lambda: got[k][...], lambda: had[k][...])
        either(take, out.at[q, count], lambda: third_got[q, 0], lambda: third[q, 0])
    for k in range(count + 1):
        m0 = dot(out[0, k], inv[0]).astype(out.dtype)
        p1 = (out[1, k].astype(jnp.float32) - dot(m0, v[...])).astype(out.dtype)
        out[0, k] = m0
        out[1, k] = dot(p1, inv[1]).astype(out.dtype)


def settle_rows(n, m, piv, l_half, sib_l, *refs):
    came, upper, lefts = refs[:-2], refs[-2], refs[-1]
    half = came[0].shape[0] // 2
    f = facts(n, m, 2, piv)
    r = f["r"]
    for which in range(2):
        place = r if which == 0 else n - 1 - r
        slot = jnp.where(f["low_first"], which, 1 - which)
        for s in range(len(came)):
            here = place == 0 if s == 0 else (place & (2 * (n >> s) - 1)) == (n >> s)

            @pl.when(here)
            def _():
                upper[slot] = came[s][...]

    lefts[rows(f["core"], half), :] = l_half[...]
    lefts[rows(1 - f["core"], half), :] = sib_l[...]
    for p in range(2):
        cut = slice(p * half, (p + 1) * half)
        fresh = upper[1, cut, :].astype(jnp.float32) - dot(lefts[cut, :], upper[0])
        upper[1, cut, :] = fresh.astype(upper.dtype)


def update(f, upper, mine, sib, at, old, new):
    half = old.shape[0] // 2
    for p in range(2):
        part = jnp.where(f["core"] == p, 0, 1)
        cut = slice(p * half, (p + 1) * half)

        def left(q):
            return jnp.where(part == 0, mine[(q, *at)], sib[(q, *at)])

        m0, m1 = left(0), left(1)

        @pl.when(f["j"] == f["c"][0])
        def _():
            new[cut, :] = m0

        @pl.when(f["j"] == f["c"][1])
        def _():
            new[cut, :] = m1

        @pl.when(jnp.logical_and(f["j"] != f["c"][0], f["j"] != f["c"][1]))
        def _():
            w = (old[cut, :].astype(jnp.float32) - dot(m0, upper[0])).astype(new.dtype)
            w = w.astype(jnp.float32) - dot(m1, upper[1])
            new[cut, :] = w.astype(new.dtype)


def finish(n, m, piv, upper, lefts, mine, sib, raw, moved, out, old, new, sems):
    rb = raw.shape[0]
    f = facts(n, m, rb, piv)
    copies = []
    for k in range(rb - 1):
        update(f, upper, mine, sib, (k,), raw.at[k], new.at[k])
        copies.append(pltpu.make_async_copy(new.at[k], out.at[f["slots"][k]], sems.at[k]))
        copies[-1].start()
    k = rb - 1
    low_first = f["low_first"]
    first = jnp.where(low_first, f["is_low"], f["is_high"])
    second = jnp.where(low_first, f["is_high"], f["is_low"])

    @pl.when(first)
    def _():
        new[k] = upper[0]

    @pl.when(second)
    def _():
        either(f["j"] == f["c"][0], new.at[k], lambda: lefts[...], lambda: upper[1])

    @pl.when(jnp.logical_not(jnp.logical_or(first, second)))
    def _():
        either(f["is_end"], old, lambda: moved[...], lambda: raw[k])
        update(f, upper, mine, sib, (k,), old, new.at[k])

    copies.append(pltpu.make_async_copy(new.at[k], out.at[f["slots"][k]], sems.at[k]))
    copies[-1].start()
    for copy in copies:
        copy.wait()


def local(matrix, pattern, inverses, pivots):
    n = lax.axis_size("prow")
    m = lax.axis_size("pcol")
    rb, width = matrix.shape[0], matrix.shape[1]
    half = width // 2
    chips = m // 2
    stages = chips.bit_length() - 1
    dt = matrix.dtype
    blocks = matrix.reshape(rb, width, width)

    def call(
        kernel, shapes, specs, *operands, scratch=(), products=0, place=VMEM, after=(), name=None
    ):
        outs = [jax.ShapeDtypeStruct(s, dt) for s in shapes]
        count = len(operands)
        scratch = [pltpu.VMEM(s, dt) if isinstance(s, tuple) else s for s in scratch]

        def body(*refs):
            kernel(n, m, *refs[:count], *refs[count + len(after) :])

        kinds = {"s": SMEM, "v": VMEM, "a": ANY}
        specs = [kinds[k] for k in specs.ljust(count, "v")] + [ANY] * len(after)
        result = pl.pallas_call(
            body,
            out_shape=outs,
            in_specs=specs,
            out_specs=[place] * len(outs),
            scratch_shapes=scratch,
            compiler_params=GRANT,
            name=name or kernel.__name__,
            cost_estimate=pl.CostEstimate(
                flops=int(products * 2 * width**3),
                bytes_accessed=sum(a.size * a.dtype.itemsize for a in operands),
                transcendentals=0,
            ),
        )(*operands, *after)
        return result if len(result) > 1 else result[0]

    def along(name, pairs, value):
        with jax.named_scope(name):
            return lax.ppermute(value, "prow", pairs)

    def sibling(name, value):
        with jax.named_scope(name):
            return lax.ppermute(value, "pcol", [(i, i ^ 1) for i in range(m)])

    def across(name, stage, value):
        pairs = []
        for i in range(m):
            bit = stage if i % 2 == 0 else stages - 1 - stage
            pairs.append((i, i ^ (2 << bit)))
        with jax.named_scope(name):
            return lax.ppermute(value, "pcol", pairs)

    square, strip = (width, width), (half, width)
    raw, leaving, other = call(
        prepare,
        [(rb, *square), square, (rb, *strip)],
        "ss",
        pivots,
        pattern.T,
        blocks,
    )
    early = sibling("sib_early", other)
    exchange = [(0, n // 2), (n - 1, n // 2 - 1), (n // 2, 0), (n // 2 - 1, n - 1)]
    moved = along("swap", exchange, leaving)

    def split(stride):
        pairs = []
        for i in range(0, n, 2 * stride):
            pairs += [(i, i + stride), (n - 1 - i, n - 1 - i - stride)]
        return pairs

    hand = lambda stride: lambda _n, _m, *refs: hand_on(n, m, stride, *refs)
    pieces = [(1, *strip)] * (2 * rb - 3) + [(2, *strip)]
    panel = call(pick, pieces, "s", pivots, raw, early)
    got = [across("stays0", 0, piece) for piece in panel]
    step = lambda _n, _m, *refs: relay(n, m, n // 2, *refs)
    other_moved, send = call(
        step, [strip, square], "", leaving, moved, name="relay", after=got
    )
    for s in range(stages - 1):
        step = lambda _n, _m, *refs: forward_all(n, m, rb, s, stages, *refs)
        panel = call(
            step,
            [(rb, *strip), (rb - 1, *strip)],
            "s",
            pivots,
            *panel,
            *got,
            name="forward_all",
            after=[send],
        )
        got = [across("stays" + str(s + 1), s + 1, part) for part in panel]

    sib_moved = sibling("sib_moved", other_moved)
    step = lambda _n, _m, *refs: forward_extra(n, m, stages - 1, stages, *refs)
    extra_here = call(
        step, [strip], "s", pivots, panel[0], got[0], name="extra_here"
    )
    stays = [*panel, *got]
    third = call(
        pick_third,
        [(2, 1, *strip)],
        "s",
        pivots,
        raw,
        early,
        moved,
        sib_moved,
        after=[extra_here],
    )
    third_got = across("third0", 0, third)

    arrived = [leaving, moved]
    stride = n // 4
    while stride:
        got = along("row" + str(stride), split(stride), send)
        arrived.append(got)
        if stride > 1:
            send = call(hand(stride), [square], "", send, got, name="hand_on_row")
        stride //= 2

    came = [extra_here]
    send = extra_here
    stride = n // 2
    while stride:
        got = along("extra_z" + str(stride), split(stride), send)
        came.append(got)
        if stride > 1:
            send = call(hand(stride), [strip], "", send, got, name="hand_on", after=[third, stays[-1]])
        stride //= 2
    for s in range(stages - 1):
        step = lambda _n, _m, *refs: forward(n, m, s, stages, *refs)
        third = call(
            step, [third.shape], "s", pivots, third, third_got, name="forward_third"
        )
        third_got = across("third" + str(s + 1), s + 1, third)
    v_half, l_half = call(
        settle_extra,
        [strip] * 2,
        "s",
        pivots,
        inverses,
        *came,
        products=0.5,
        after=[third, arrived[2]],
    )
    sib_v = sibling("sib_v", v_half)
    sib_l = sibling("sib_l", l_half)
    step = lambda _n, _m, *refs: multiply(n, m, stages, *refs)
    mine = call(
        step,
        [(2, rb, *strip)],
        "s",
        pivots,
        inverses,
        v_half,
        sib_v,
        *stays,
        third,
        third_got,
        scratch=[square],
        products=3 * rb / 2,
        name="multiply",
        after=[sib_l],
    )
    sib_mine = sibling("sib_mine", mine)
    upper, lefts = call(
        settle_rows,
        [(2, *square), square],
        "s",
        pivots,
        l_half,
        sib_l,
        *arrived,
        products=1,
        after=[mine],
    )
    result = call(
        finish,
        [blocks.shape],
        "s",
        pivots,
        upper,
        lefts,
        mine,
        sib_mine,
        raw,
        moved,
        scratch=[square, (rb, *square), pltpu.SemaphoreType.DMA((rb,))],
        products=2 * rb,
        place=ANY,
    )
    return result.reshape(matrix.shape)


def solution(mesh):
    placed = (P(None, "prow", None, "pcol"), P(), P(), P())
    return jax.shard_map(
        local, mesh=mesh, in_specs=placed, out_specs=P(None, "prow", None, "pcol"), check_vma=False
    )
```

```python
import functools

import jax
import jax.numpy as jnp
from jax import lax
from jax.experimental import pallas as pl
from jax.experimental.pallas import tpu as pltpu
from jax.sharding import PartitionSpec as P

SMEM = pl.BlockSpec(memory_space=pltpu.SMEM)
VMEM = pl.BlockSpec(memory_space=pltpu.VMEM)
ANY = pl.BlockSpec(memory_space=pl.ANY)
GRANT = pltpu.CompilerParams(vmem_limit_bytes=24 * 2**20)


def facts(n, m, rb, pivots):
    f = {}
    r = f["r"] = lax.axis_index("prow").astype(jnp.int32)
    j = f["j"] = lax.axis_index("pcol").astype(jnp.int32)
    f["core"] = j & 1
    f["chip"] = j >> 1
    low_first = f["low_first"] = pivots[0, 1] == 0
    shift = n.bit_length() - 1
    a_low = jnp.where(low_first, pivots[0, 0], pivots[1, 0]) >> shift
    a_high = jnp.where(low_first, pivots[1, 0], pivots[0, 0]) >> shift
    f["c"] = [pivots[0, 2], pivots[1, 2]]
    is_low, is_high = r == n // 2, r == n // 2 - 1
    f["is_low"], f["is_high"] = is_low, is_high
    f["is_end"] = jnp.logical_or(r == 0, r == n - 1)
    out = jnp.where(is_low, a_low, jnp.where(is_high, a_high, jnp.where(r == 0, 0, rb - 1)))
    f["slots"] = []
    for k in range(rb):
        slot = out + (1 + k)
        f["slots"].append(jnp.where(slot >= rb, slot - rb, slot))
    f["cx"] = jnp.where((r == 0) == low_first, pivots[1, 2], pivots[0, 2])
    return f


def either(cond, out_ref, yes, no):
    @pl.when(cond)
    def _():
        out_ref[...] = yes()

    @pl.when(jnp.logical_not(cond))
    def _():
        out_ref[...] = no()


def rows(part, half):
    return pl.ds(pl.multiple_of(part * half, half), half)


def prepare(n, m, piv, pat, mat, raw, leaving, other):
    rb, width = mat.shape[0], mat.shape[1]
    f = facts(n, m, rb, piv)
    cut = rows(1 - f["core"], width // 2)
    for k in reversed(range(rb)):
        slot = f["slots"][k]
        keep = pat[f["j"], slot * n + f["r"]] != 0
        zero = lambda: jnp.zeros((width, width), mat.dtype)
        either(keep, raw.at[k], lambda: mat[slot], zero)
        if k == rb - 1:
            leaving[...] = raw[k]
        other[k] = raw[k, cut, :]


def views(refs, rb):
    if refs[0].shape[0] == rb:
        one = [refs[0].at[k] for k in range(rb)] + [refs[1].at[k] for k in range(rb - 1)]
        return one[0], one[1:rb], one[rb:]
    one = [ref.at[0] for ref in refs]
    return refs[-1].at[1], one[: rb - 1], one[rb - 1 :]


def pick(n, m, piv, raw, sib, *pieces):
    rb, width = raw.shape[0], raw.shape[1]
    f = facts(n, m, rb, piv)
    cut = rows(f["core"], width // 2)
    extra, *panel = views(pieces, rb)
    hit = (f["cx"] & 1) == f["core"]
    either(hit, extra, lambda: raw[rb - 1, cut, :], lambda: sib[rb - 1])
    for q in range(2):
        hit = (f["c"][q] & 1) == f["core"]
        for k in range(rb - 1):
            either(hit, panel[q][k], lambda: raw[k, cut, :], lambda: sib[k])


def pick_third(n, m, piv, raw, sib, moved, sib_moved, panel):
    rb, width = raw.shape[0], raw.shape[1]
    f = facts(n, m, rb, piv)
    cut = rows(f["core"], width // 2)
    for q in range(2):
        hit = (f["c"][q] & 1) == f["core"]

        @pl.when(f["is_end"])
        def _():
            either(hit, panel.at[q, 0], lambda: moved[cut, :], lambda: sib_moved[...])

        @pl.when(jnp.logical_not(f["is_end"]))
        def _():
            either(hit, panel.at[q, 0], lambda: raw[rb - 1, cut, :], lambda: sib[rb - 1])


def relay(n, m, moved, other, send):
    core = lax.axis_index("pcol").astype(jnp.int32) & 1
    other[...] = moved[rows(1 - core, moved.shape[0] // 2), :]
    send[...] = moved[...]


def bit_of(f, column, stage, stages):
    apart = f["chip"] ^ (column >> 1)
    bit = jnp.where(f["core"] == 0, stage, stages - 1 - stage)
    return ((apart >> bit) & 1) == 1


def forward_extra(n, m, stage, stages, piv, had, got, out):
    f = facts(n, m, 2, piv)
    take = bit_of(f, f["cx"], stage, stages)
    either(take, out, lambda: got[0], lambda: had[0])


def forward(n, m, stage, stages, piv, had, got, out):
    f = facts(n, m, 2, piv)
    for q in range(2):
        take = bit_of(f, f["c"][q], stage, stages)
        either(take, out.at[q], lambda: got[q], lambda: had[q])


def forward_all(n, m, rb, stage, stages, piv, *refs):
    f = facts(n, m, 2, piv)
    count = (len(refs) - 2) // 2
    had, got = views(refs[:count], rb), views(refs[count:-2], rb)
    out = views(refs[-2:], rb)
    take = bit_of(f, f["cx"], stage, stages)
    either(take, out[0], lambda: got[0][...], lambda: had[0][...])
    for q in range(2):
        take = bit_of(f, f["c"][q], stage, stages)
        for k in range(rb - 1):
            either(take, out[1 + q][k], lambda: got[1 + q][k][...], lambda: had[1 + q][k][...])


def hand_on(n, m, stride, had, got, extra):
    r = lax.axis_index("prow").astype(jnp.int32)
    low = (r & (2 * stride - 1)) == stride
    high = ((n - 1 - r) & (2 * stride - 1)) == stride
    either(jnp.logical_or(low, high), extra, lambda: got[...], lambda: had[...])


def dot(left, right):
    return jnp.dot(left, right, preferred_element_type=jnp.float32)


def settle_extra(n, m, piv, inv, *refs):
    had, out = refs[:-2], refs[-2:]
    f = facts(n, m, 2, piv)
    r = f["r"]
    stages = len(had) - 1
    for which in range(2):
        place = r if which == 0 else n - 1 - r
        low_is_v = f["low_first"] if which == 0 else jnp.logical_not(f["low_first"])
        for s in range(stages + 1):
            if s == 0:
                here = place == 0
            else:
                here = (place & (2 * (n >> s) - 1)) == (n >> s)

            @pl.when(jnp.logical_and(here, low_is_v))
            def _():
                out[0][...] = had[s][...]

            @pl.when(jnp.logical_and(here, jnp.logical_not(low_is_v)))
            def _():
                out[1][...] = had[s][...]

    out[1][...] = dot(out[1][...], inv[0]).astype(out[1].dtype)


def multiply(n, m, stages, piv, inv, v_half, sib_v, *refs):
    panels, third, third_got, out, v = refs[:-4], refs[-4], refs[-3], refs[-2], refs[-1]
    f = facts(n, m, 2, piv)
    half = v_half.shape[0]
    v[rows(f["core"], half), :] = v_half[...]
    v[rows(1 - f["core"], half), :] = sib_v[...]
    count = out.shape[1] - 1
    for q in range(2):
        take = bit_of(f, f["c"][q], stages - 1, stages)
        had, got = (views(panels[i : i + 2], count + 1)[1 + q] for i in (0, 2))
        for k in range(count):
            either(take, out.at[q, k], lambda: got[k][...], lambda: had[k][...])
        either(take, out.at[q, count], lambda: third_got[q, 0], lambda: third[q, 0])
    for k in range(count + 1):
        m0 = dot(out[0, k], inv[0]).astype(out.dtype)
        p1 = (out[1, k].astype(jnp.float32) - dot(m0, v[...])).astype(out.dtype)
        out[0, k] = m0
        out[1, k] = dot(p1, inv[1]).astype(out.dtype)


def settle_rows(n, m, piv, l_half, sib_l, *refs):
    came, upper, lefts = refs[:-2], refs[-2], refs[-1]
    half = came[0].shape[0] // 2
    f = facts(n, m, 2, piv)
    r = f["r"]
    for which in range(2):
        place = r if which == 0 else n - 1 - r
        slot = jnp.where(f["low_first"], which, 1 - which)
        for s in range(len(came)):

            @pl.when(place == s)
            def _():
                upper[slot] = came[s][...]

    lefts[rows(f["core"], half), :] = l_half[...]
    lefts[rows(1 - f["core"], half), :] = sib_l[...]
    for p in range(2):
        cut = slice(p * half, (p + 1) * half)
        fresh = upper[1, cut, :].astype(jnp.float32) - dot(lefts[cut, :], upper[0])
        upper[1, cut, :] = fresh.astype(upper.dtype)


def update(f, upper, mine, sib, at, old, new):
    half = old.shape[0] // 2
    for p in range(2):
        part = jnp.where(f["core"] == p, 0, 1)
        cut = slice(p * half, (p + 1) * half)

        def left(q):
            return jnp.where(part == 0, mine[(q, *at)], sib[(q, *at)])

        m0, m1 = left(0), left(1)

        @pl.when(f["j"] == f["c"][0])
        def _():
            new[cut, :] = m0

        @pl.when(f["j"] == f["c"][1])
        def _():
            new[cut, :] = m1

        @pl.when(jnp.logical_and(f["j"] != f["c"][0], f["j"] != f["c"][1]))
        def _():
            w = (old[cut, :].astype(jnp.float32) - dot(m0, upper[0])).astype(new.dtype)
            w = w.astype(jnp.float32) - dot(m1, upper[1])
            new[cut, :] = w.astype(new.dtype)


def finish(n, m, piv, upper, lefts, mine, sib, raw, moved, out, old, new, sems):
    rb = raw.shape[0]
    f = facts(n, m, rb, piv)
    copies = []
    for k in range(rb - 1):
        update(f, upper, mine, sib, (k,), raw.at[k], new.at[k])
        copies.append(pltpu.make_async_copy(new.at[k], out.at[f["slots"][k]], sems.at[k]))
        copies[-1].start()
    k = rb - 1
    low_first = f["low_first"]
    first = jnp.where(low_first, f["is_low"], f["is_high"])
    second = jnp.where(low_first, f["is_high"], f["is_low"])

    @pl.when(first)
    def _():
        new[k] = upper[0]

    @pl.when(second)
    def _():
        either(f["j"] == f["c"][0], new.at[k], lambda: lefts[...], lambda: upper[1])

    @pl.when(jnp.logical_not(jnp.logical_or(first, second)))
    def _():
        either(f["is_end"], old, lambda: moved[...], lambda: raw[k])
        update(f, upper, mine, sib, (k,), old, new.at[k])

    copies.append(pltpu.make_async_copy(new.at[k], out.at[f["slots"][k]], sems.at[k]))
    copies[-1].start()
    for copy in copies:
        copy.wait()


def local(matrix, pattern, inverses, pivots):
    n = lax.axis_size("prow")
    m = lax.axis_size("pcol")
    rb, width = matrix.shape[0], matrix.shape[1]
    half = width // 2
    chips = m // 2
    stages = chips.bit_length() - 1
    dt = matrix.dtype
    blocks = matrix.reshape(rb, width, width)

    def call(
        kernel, shapes, specs, *operands, scratch=(), products=0, place=VMEM, after=(), name=None
    ):
        outs = [jax.ShapeDtypeStruct(s, dt) for s in shapes]
        count = len(operands)
        scratch = [pltpu.VMEM(s, dt) if isinstance(s, tuple) else s for s in scratch]

        def body(*refs):
            kernel(n, m, *refs[:count], *refs[count + len(after) :])

        kinds = {"s": SMEM, "v": VMEM, "a": ANY}
        specs = [kinds[k] for k in specs.ljust(count, "v")] + [ANY] * len(after)
        result = pl.pallas_call(
            body,
            out_shape=outs,
            in_specs=specs,
            out_specs=[place] * len(outs),
            scratch_shapes=scratch,
            compiler_params=GRANT,
            name=name or kernel.__name__,
            cost_estimate=pl.CostEstimate(
                flops=int(products * 2 * width**3),
                bytes_accessed=sum(a.size * a.dtype.itemsize for a in operands),
                transcendentals=0,
            ),
        )(*operands, *after)
        return result if len(result) > 1 else result[0]

    def along(name, pairs, value):
        with jax.named_scope(name):
            return lax.ppermute(value, "prow", pairs)

    def sibling(name, value):
        with jax.named_scope(name):
            return lax.ppermute(value, "pcol", [(i, i ^ 1) for i in range(m)])

    def across(name, stage, value):
        pairs = []
        for i in range(m):
            bit = stage if i % 2 == 0 else stages - 1 - stage
            pairs.append((i, i ^ (2 << bit)))
        with jax.named_scope(name):
            return lax.ppermute(value, "pcol", pairs)

    square, strip = (width, width), (half, width)
    raw, leaving, other = call(
        prepare,
        [(rb, *square), square, (rb, *strip)],
        "ss",
        pivots,
        pattern.T,
        blocks,
    )
    early = sibling("sib_early", other)
    exchange = [(0, 1), (n - 1, n - 2), (n // 2, 0), (n // 2 - 1, n - 1)]
    moved = along("swap", exchange, leaving)

    def split(stride):
        pairs = []
        for i in range(0, n, 2 * stride):
            pairs += [(i, i + stride), (n - 1 - i, n - 1 - i - stride)]
        return pairs

    hand = lambda stride: lambda _n, _m, *refs: hand_on(n, m, stride, *refs)
    pieces = [(1, *strip)] * (2 * rb - 3) + [(2, *strip)]
    panel = call(pick, pieces, "s", pivots, raw, early)
    got = [across("stays0", 0, piece) for piece in panel]
    other_moved, send = call(relay, [strip, square], "", moved, name="relay", after=got)
    for s in range(stages - 1):
        step = lambda _n, _m, *refs: forward_all(n, m, rb, s, stages, *refs)
        panel = call(
            step,
            [(rb, *strip), (rb - 1, *strip)],
            "s",
            pivots,
            *panel,
            *got,
            name="forward_all",
            after=[send],
        )
        got = [across("stays" + str(s + 1), s + 1, part) for part in panel]

    sib_moved = sibling("sib_moved", other_moved)
    step = lambda _n, _m, *refs: forward_extra(n, m, stages - 1, stages, *refs)
    extra_here = call(
        step, [strip], "s", pivots, panel[0], got[0], name="extra_here"
    )
    stays = [*panel, *got]
    third = call(
        pick_third,
        [(2, 1, *strip)],
        "s",
        pivots,
        raw,
        early,
        moved,
        sib_moved,
        after=[extra_here],
    )
    third_got = across("third0", 0, third)

    arrived = [leaving, moved]
    for h in range(1, n - 1):
        send = along("row" + str(h), [(h, h + 1), (n - 1 - h, n - 2 - h)], send)
        arrived.append(send)

    came = [extra_here]
    send = extra_here
    stride = n // 2
    while stride:
        got = along("extra_z" + str(stride), split(stride), send)
        came.append(got)
        if stride > 1:
            send = call(hand(stride), [strip], "", send, got, name="hand_on", after=[third, stays[-1], arrived[2]])
        stride //= 2
    for s in range(stages - 1):
        step = lambda _n, _m, *refs: forward(n, m, s, stages, *refs)
        third = call(
            step, [third.shape], "s", pivots, third, third_got, name="forward_third"
        )
        third_got = across("third" + str(s + 1), s + 1, third)
    v_half, l_half = call(
        settle_extra,
        [strip] * 2,
        "s",
        pivots,
        inverses,
        *came,
        products=0.5,
        after=[third, arrived[3]],
    )
    sib_v = sibling("sib_v", v_half)
    sib_l = sibling("sib_l", l_half)
    step = lambda _n, _m, *refs: multiply(n, m, stages, *refs)
    mine = call(
        step,
        [(2, rb, *strip)],
        "s",
        pivots,
        inverses,
        v_half,
        sib_v,
        *stays,
        third,
        third_got,
        scratch=[square],
        products=3 * rb / 2,
        name="multiply",
        after=[sib_l],
    )
    sib_mine = sibling("sib_mine", mine)
    upper, lefts = call(
        settle_rows,
        [(2, *square), square],
        "s",
        pivots,
        l_half,
        sib_l,
        *arrived,
        products=1,
        after=[mine],
    )
    result = call(
        finish,
        [blocks.shape],
        "s",
        pivots,
        upper,
        lefts,
        mine,
        sib_mine,
        raw,
        moved,
        scratch=[square, (rb, *square), pltpu.SemaphoreType.DMA((rb,))],
        products=2 * rb,
        place=ANY,
    )
    return result.reshape(matrix.shape)


def solution(mesh):
    placed = (P(None, "prow", None, "pcol"), P(), P(), P())
    return jax.shard_map(
        local, mesh=mesh, in_specs=placed, out_specs=P(None, "prow", None, "pcol"), check_vma=False
    )
```
